32 devices in a mesh: front: 8 (over z, x), col: 4 (over y, core).
Axes of the slice: x: 2, y: 2, z: 4, core: 2. Of those that a mesh axis runs over, the one named last changes fastest.
Arguments:
- leaf_load: bfloat16 [8192, 2048], P('front', 'col'), may hold values from -6 to 6
- leaf_inverse: bfloat16 [8192, 1024], P(('front', 'col')), may hold values from -0.1875 to 0.1875
- leaf_coupling: bfloat16 [4096, 1024], P('front'), may hold values from -0.1875 to 0.1875
- leaf_rowmap: int32 [8, 512], P('front'), may hold values from 0 to 511, each once within a row
- load_first: bfloat16 [2048, 2048], P('front', 'col'), may hold values from -6 to 6
- load_second: bfloat16 [1024, 2048], P('front', 'col'), may hold values from -6 to 6
- load_third: bfloat16 [512, 2048], P('front', 'col'), may hold values from -6 to 6
- inverse_first: bfloat16 [2048, 512], P('front'), may hold values from -0.15625 to 0.15625
- inverse_second: bfloat16 [1024, 512], P('front'), may hold values from -0.15625 to 0.15625
- inverse_third: bfloat16 [512, 512], P('front'), may hold values from -0.15625 to 0.15625
- coupling_first: bfloat16 [512, 2048], P(None, 'front'), may hold values from -0.25 to 0.25
- coupling_second: bfloat16 [512, 1024], P(None, 'front'), may hold values from -0.25 to 0.25
- rowmap_first: int32 [4, 512], replicated, may hold values from 0 to 511, each once within a row
- rowmap_second: int32 [2, 512], replicated, may hold values from 0 to 511, each once within a row
- surface_coupling: bfloat16 [24, 1024, 1024], P('front'), may hold values from -0.125 to 0.125
- neighbor_tiles: int32 [8, 2], replicated, may hold values from 0 to 7, as said below
Outputs:
- volume_solution: bfloat16 [8192, 2048], P('front', 'col')
- surface_tiles: bfloat16 [8192, 2048], P('front', 'col')
- solution_first: bfloat16 [2048, 2048], P('front', 'col')
- solution_second: bfloat16 [1024, 2048], P('front', 'col')
- solution_third: bfloat16 [512, 2048], P('front', 'col')
The draws below stay inside these ranges and needn't reach their ends.
Inputs may be any that keep to these rules, and one draw needn't show every extreme that they name: Each row of leaf_rowmap is a permutation of the 512 separator rows. Each row of rowmap_first is a permutation of the 512 separator rows. Each row of rowmap_second is a permutation of the 512 separator rows. `neighbor_tiles`: row f names two different tiles, neither equal to f, each within 2 of f; counting each front's own tile, every tile receives 1 to 5 contributions, and some tile receives 5.
All inputs are finite; a program needn't handle non-finite values.
Results may differ from the reference program's by a relative error of at most 0.015.
Values may be sent and summed in bfloat16 or wider, within the bound.
A program may use at most 128 MiB of HBM per device.

```python
import jax
import jax.numpy as jnp
from jax import lax

F = 1024
S = 512
TR = 1024
PANEL = 2048
N_FRONT = 8


def draw_neighbor_tiles(key, part):
    center_key, score_key = jax.random.split(jax.random.fold_in(key, 11))
    offsets = jnp.array([-2, -1, 1, 2], jnp.int32)
    fronts = jnp.arange(N_FRONT, dtype=jnp.int32)
    target = fronts[:, None] + offsets[None, :]
    center = jax.random.randint(center_key, (), 2, N_FRONT - 2).astype(jnp.int32)
    scores = jax.random.randint(score_key, (N_FRONT, 4), 0, 1000).astype(jnp.int32) * 4 + jnp.arange(4, dtype=jnp.int32)[None, :]
    scores = jnp.where((target < 0) | (target >= N_FRONT), scores + 100000, scores)
    scores = jnp.where(target == center, scores - 100000, scores)
    ranking = jnp.argsort(scores, axis=1)[:, :2]
    return jnp.take_along_axis(target, ranking, axis=1).astype(jnp.int32)


def block_levels(key, shape, cuts, low, top_value):
    def one(position, blocks):
        heights = jax.random.uniform(jax.random.fold_in(jax.random.fold_in(key, 6), position), (blocks,), jnp.float32, low / len(cuts), top_value / len(cuts))
        return jnp.repeat(jnp.exp(heights), shape[position] // blocks).reshape((-1,) + (1,) * (len(shape) - position - 1))

    gain = one(*cuts[0])
    for cut in cuts[1:]:
        gain = gain * one(*cut)
    return gain


def normal_values(key, dims, scale, reach, cuts=(), held_as=jnp.bfloat16):
    entries = scale * jax.random.normal(key, dims, jnp.float32)
    if cuts:
        entries = entries * block_levels(key, dims, cuts, -0.22, 0.18)
    return jnp.clip(entries, -reach, reach).astype(held_as)


def setup_inputs(seed: int = 0) -> dict:
    streams_of = jax.random.split(jax.random.key(seed), 17)
    return {
        "leaf_load": normal_values(streams_of[0], (N_FRONT * F, PANEL), 1.0, 6.0, ((0, 8), (1, 4))),
        "leaf_inverse": normal_values(streams_of[1], (N_FRONT * F, F), F ** -0.5, 0.1875, ((0, 32),)),
        "leaf_coupling": normal_values(streams_of[2], (N_FRONT * S, F), F ** -0.5, 0.1875, ((0, 8),)),
        "leaf_rowmap": jax.vmap(lambda own: jax.random.permutation(own, S))(jax.random.split(streams_of[3], N_FRONT)).reshape((N_FRONT, S)).astype(jnp.int32),
        "load_first": normal_values(streams_of[4], (N_FRONT // 2 * S, PANEL), 1.0, 6.0, ((0, 8), (1, 4))),
        "load_second": normal_values(streams_of[5], (N_FRONT // 4 * S, PANEL), 1.0, 6.0, ((0, 8), (1, 4))),
        "load_third": normal_values(streams_of[6], (N_FRONT // 8 * S, PANEL), 1.0, 6.0, ((0, 8), (1, 4))),
        "inverse_first": normal_values(streams_of[7], (N_FRONT // 2 * S, S), (3 * S) ** -0.5, 0.15625, ((0, 8),)),
        "inverse_second": normal_values(streams_of[8], (N_FRONT // 4 * S, S), (3 * S) ** -0.5, 0.15625, ((0, 8),)),
        "inverse_third": normal_values(streams_of[9], (N_FRONT // 8 * S, S), (3 * S) ** -0.5, 0.15625, ((0, 8),)),
        "coupling_first": normal_values(streams_of[10], (S, N_FRONT // 2 * S), S ** -0.5, 0.25, ((1, 8),)),
        "coupling_second": normal_values(streams_of[11], (S, N_FRONT // 4 * S), S ** -0.5, 0.25, ((1, 8),)),
        "rowmap_first": jax.vmap(lambda own: jax.random.permutation(own, S))(jax.random.split(streams_of[12], (N_FRONT // 2))).reshape((N_FRONT // 2, S)).astype(jnp.int32),
        "rowmap_second": jax.vmap(lambda own: jax.random.permutation(own, S))(jax.random.split(streams_of[13], (N_FRONT // 4))).reshape((N_FRONT // 4, S)).astype(jnp.int32),
        "surface_coupling": normal_values(streams_of[14], (N_FRONT * 3, TR, F), (2 * F) ** -0.5, 0.125, ((0, 8),)),
        "neighbor_tiles": draw_neighbor_tiles(jax.random.fold_in(streams_of[16], 71), 0),
    }


def products(left, right):
    return lax.map(lambda operands: jnp.dot(operands[0], operands[1], preferred_element_type=jnp.float32), (left, right))


def transposed(left, right):
    return lax.map(lambda operands: jnp.dot(operands[0].T, operands[1], preferred_element_type=jnp.float32), (left, right))


def gathered(values, rowmap):
    return jax.vmap(lambda current, row_index: current[row_index])(values, rowmap)


def scattered(values, rowmap):
    return jax.vmap(lambda current, row_index: jnp.zeros_like(current).at[row_index].set(current))(values, rowmap)


def slot_products(operands):
    surface, volume = operands
    return jnp.stack([jnp.dot(surface[slot], volume, preferred_element_type=jnp.float32) for slot in range(3)])


def reference(leaf_load, leaf_inverse, leaf_coupling, leaf_rowmap, load_first, load_second, load_third, inverse_first, inverse_second, inverse_third, coupling_first, coupling_second, rowmap_first, rowmap_second, surface_coupling, neighbor_tiles):
    fronts = leaf_load.shape[0] // F
    panel_cols = leaf_load.shape[1]
    leaf_right = leaf_load.reshape(fronts, F, panel_cols)
    leaf_factor = leaf_inverse.reshape(fronts, F, F)
    leaf_links = leaf_coupling.reshape(fronts, S, F)
    leaf_start = products(leaf_factor, leaf_right).astype(jnp.bfloat16)
    partial_value = gathered(products(leaf_links, leaf_start), leaf_rowmap)
    load_list = (load_first, load_second, load_third)
    inverses = (inverse_first, inverse_second, inverse_third)
    couplings = (coupling_first, coupling_second)
    rowmaps = (rowmap_first, rowmap_second)
    solved = []
    node_count = fronts
    for level_index in range(3):
        node_count = node_count // 2
        load_rows = load_list[level_index].reshape(node_count, S, panel_cols).astype(jnp.float32)
        right_side = (load_rows - partial_value[0::2] - partial_value[1::2]).astype(jnp.bfloat16)
        inverse = inverses[level_index].reshape(node_count, S, S)
        solution = products(inverse, right_side).astype(jnp.bfloat16)
        solved.append(solution)
        if level_index < 2:
            coupling = couplings[level_index].reshape(S, node_count, S).transpose(1, 0, 2)
            partial_value = gathered(products(coupling, solution), rowmaps[level_index])
    parent_rows = solved[2]
    results = [None, None, parent_rows]
    for level_index in (1, 0):
        node_count = solved[level_index].shape[0]
        lifted = scattered(jnp.repeat(parent_rows, 2, axis=0), rowmaps[level_index])
        coupling = couplings[level_index].reshape(S, node_count, S).transpose(1, 0, 2)
        pulled = transposed(coupling, lifted).astype(jnp.bfloat16)
        inverse = inverses[level_index].reshape(node_count, S, S)
        parent_rows = (solved[level_index].astype(jnp.float32) - products(inverse, pulled)).astype(jnp.bfloat16)
        results[level_index] = parent_rows
    lifted = scattered(jnp.repeat(parent_rows, 2, axis=0), leaf_rowmap)
    pulled = transposed(leaf_links, lifted).astype(jnp.bfloat16)
    volume = (leaf_start.astype(jnp.float32) - products(leaf_factor, pulled)).astype(jnp.bfloat16)
    surface = surface_coupling.reshape(fronts, 3, TR, F)
    contribution = lax.map(slot_products, (surface, volume)).astype(jnp.bfloat16)
    own_tiles = jnp.arange(fronts, dtype=jnp.int32)[:, None]
    destination = jnp.concatenate([own_tiles, neighbor_tiles.astype(jnp.int32)], axis=1).reshape(-1)
    tile_sums = jnp.zeros((fronts, TR, panel_cols), jnp.float32).at[destination].add(contribution.reshape(fronts * 3, TR, panel_cols).astype(jnp.float32))
    return (volume.reshape(fronts * F, panel_cols), tile_sums.astype(jnp.bfloat16).reshape(fronts * TR, panel_cols), results[0].reshape(-1, panel_cols), results[1].reshape(-1, panel_cols), results[2].reshape(-1, panel_cols))
```

```python
import jax
import jax.numpy as jnp
from jax import lax
from jax.sharding import PartitionSpec as P

BF = jnp.bfloat16
F32 = jnp.float32


def swap(x, bit):
    n = lax.axis_size("front")
    return lax.ppermute(x, "front", [(i, i ^ (1 << bit)) for i in range(n)])


def shifted(x, step):
    n = lax.axis_size("front")
    return lax.ppermute(
        x, "front", [(i, i + step) for i in range(max(0, -step), min(n, n - step))]
    )


def family(x, bits, axis):
    n = lax.axis_size("front")
    size = 1 << bits
    groups = [list(range(g, g + size)) for g in range(0, n, size)]
    return lax.all_gather(x, "front", axis=axis, tiled=True, axis_index_groups=groups)


def mm(a, b):
    return jnp.dot(a, b, preferred_element_type=F32)


def tmm(a, b):
    return lax.dot_general(a, b, (((0,), (0,)), ((), ())), preferred_element_type=F32)


def columns(x, bit):
    half = x.shape[1] // 2
    upper = (lax.axis_index("front") >> bit) & 1 == 1
    low, high = x[:, :half], x[:, half:]
    return jnp.where(upper, high, low), jnp.where(upper, low, high)


def rejoin(mine, other, bit):
    upper = (lax.axis_index("front") >> bit) & 1 == 1
    return jnp.where(
        upper,
        jnp.concatenate([other, mine], axis=1),
        jnp.concatenate([mine, other], axis=1),
    )


def local(
    leaf_load, leaf_inverse, leaf_coupling, leaf_rowmap,
    load_first, load_second, load_third,
    inverse_first, inverse_second, inverse_third,
    coupling_first, coupling_second, rowmap_first, rowmap_second,
    surface_coupling, neighbor_tiles,
):
    me = lax.axis_index("front")
    n = lax.axis_size("front")
    factor = lax.all_gather(leaf_inverse, "col", axis=0, tiled=True)
    inv1 = family(inverse_first, 1, 0)
    inv2 = family(inverse_second, 2, 0)
    inv3 = family(inverse_third, 3, 0)
    d_mat = family(coupling_first, 1, 1)
    e_mat = family(coupling_second, 2, 1)
    row1 = lax.dynamic_index_in_dim(rowmap_first, me >> 1, 0, keepdims=False)
    row2 = lax.dynamic_index_in_dim(rowmap_second, me >> 2, 0, keepdims=False)
    c_mat = leaf_coupling[leaf_rowmap[0]]
    d_mat = d_mat[row1]
    e_mat = e_mat[row2]
    load1 = family(load_first, 1, 0)
    load2 = family(load_second, 2, 0)
    load3 = family(load_third, 3, 0)

    start = mm(factor, leaf_load).astype(BF)
    part = mm(c_mat, start).astype(BF)
    keep, give = columns(part, 0)
    l1, _ = columns(load1, 0)
    rhs1 = (l1.astype(F32) - keep.astype(F32) - swap(give, 0).astype(F32)).astype(BF)
    y1 = mm(inv1, rhs1).astype(BF)
    part = mm(d_mat, y1).astype(BF)
    keep, give = columns(part, 1)
    l2, _ = columns(columns(load2, 0)[0], 1)
    rhs2 = (l2.astype(F32) - keep.astype(F32) - swap(give, 1).astype(F32)).astype(BF)
    y2 = mm(inv2, rhs2).astype(BF)
    part = mm(e_mat, y2).astype(BF)
    l3, _ = columns(columns(load3, 0)[0], 1)
    rhs3 = (l3.astype(F32) - part.astype(F32) - swap(part, 2).astype(F32)).astype(BF)
    s3 = mm(inv3, rhs3).astype(BF)
    pull2 = tmm(e_mat, s3).astype(BF)
    s2 = (y2.astype(F32) - mm(inv2, pull2)).astype(BF)
    both = jnp.concatenate([s2, s3], axis=0)
    both = rejoin(both, swap(both, 1), 1)
    sep = s2.shape[0]
    pull1 = tmm(d_mat, both[:sep]).astype(BF)
    s1 = (y1.astype(F32) - mm(inv1, pull1)).astype(BF)
    full = jnp.concatenate([s1, both], axis=0)
    full = rejoin(full, swap(full, 0), 0)
    s1 = full[:sep]
    pulled = tmm(c_mat, s1).astype(BF)
    volume = (start.astype(F32) - mm(factor, pulled)).astype(BF)

    def rows_of(x, bits, like):
        r = like.shape[0]
        return lax.dynamic_slice_in_dim(x, (me % (1 << bits)) * r, r, 0)

    out1 = rows_of(s1, 1, load_first)
    out2 = rows_of(full[sep : 2 * sep], 2, load_second)
    out3 = rows_of(full[2 * sep :], 3, load_third)

    own = lax.dynamic_index_in_dim(neighbor_tiles, me, 0, keepdims=False)
    first = mm(surface_coupling[1], volume).astype(BF)
    second = mm(surface_coupling[2], volume).astype(BF)
    zero = jnp.zeros_like(first)
    arrived = []
    for step in (-1, 1, -2, 2):
        dest = me + step
        block = jnp.where(own[0] == dest, first, jnp.where(own[1] == dest, second, zero))
        arrived.append(shifted(block, step))
    total = mm(surface_coupling[0], volume).astype(BF).astype(F32)
    for block in arrived:
        total = total + block.astype(F32)
    return volume, total.astype(BF), out1, out2, out3


def solution(mesh):
    return jax.shard_map(
        local,
        mesh=mesh,
        in_specs=(
            P("front", "col"), P(("front", "col"), None), P("front", None), P("front", None),
            P("front", "col"), P("front", "col"), P("front", "col"),
            P("front", None), P("front", None), P("front", None),
            P(None, "front"), P(None, "front"), P(), P(),
            P("front", None, None), P(),
        ),
        out_specs=(P("front", "col"),) * 5,
        check_vma=False,
    )
```

```python
import functools

import jax
import jax.numpy as jnp
from jax import lax
from jax.experimental import pallas as pl
from jax.experimental.pallas import tpu as pltpu
from jax.sharding import PartitionSpec as P

BF = jnp.bfloat16
F32 = jnp.float32
MESH = pl.DeviceIdType.MESH
OFFSETS = (-1, 1, -2, 2)


def mm(a, b):
    return jnp.dot(a, b, preferred_element_type=F32)


def tmm(a, b):
    return lax.dot_general(a, b, (((0,), (0,)), ((), ())), preferred_element_type=F32)


def flip(x, bit):
    return x + bit * (1 - 2 * ((x // bit) % 2))


def rotated(x, size, step):
    return (x // size) * size + (x % size + step) % size


def kernel(
    n, b_ref, g_ref, c_ref, map0, l1, l2, l3, i1, i2, i3, d_ref, e_ref, map1, map2, tile_ref, a_hbm,
    vol, tiles, o1, o2, o3,
    gf, ct, start, part, w1, w2, w3, l1f, l2f, l3f,
    give1, x1, y1, p2, give2, x2, y2, p3, x3, s3, s2, s1, o3s, o2s, pull, av, stage, got,
    send_sem, recv_sem, tile_send, tile_recv, a_sem,
):
    f = lax.axis_index("front")
    c = lax.axis_index("col")
    core = c % 2
    ca, cb = flip(c, 1), flip(c, 2)
    cd = flip(ca, 2)
    b0, b1 = f % 2, (f // 2) % 2
    fx, fy, fz = flip(f, 1), flip(f, 2), flip(f, 4)
    sep = l1f.shape[0]
    panel = b_ref.shape[1]
    half, quarter = panel // 2, panel // 4
    block = g_ref.shape[0]
    r1, r2, r3 = i1.shape[0], i2.shape[0], i3.shape[0]

    def cols(at, size):
        return pl.ds(pl.multiple_of(at, 128), size)

    def rows(at, size):
        return pl.ds(pl.multiple_of(at, 16), size)

    def quarter_of(g):
        return cols((g % 2) * half + ((g // 2) % 2) * quarter, quarter)

    copies = []

    def send(src, dst, **where):
        i = len(copies)
        copy = pltpu.make_async_remote_copy(
            src_ref=src, dst_ref=dst, send_sem=send_sem.at[i], recv_sem=recv_sem.at[i],
            device_id=where, device_id_type=MESH,
        )
        copies.append(copy)
        copy.start()
        return copy

    load_a = pltpu.make_async_copy(a_hbm, av, a_sem)
    load_a.start()

    barrier = pltpu.get_barrier_semaphore()
    count = 9
    for other in (ca, cb):
        pl.semaphore_signal(barrier, inc=1, device_id={"col": other}, device_id_type=MESH)
    for k in range(1, 8):
        pl.semaphore_signal(
            barrier, inc=1, device_id={"front": rotated(f, 8, k)}, device_id_type=MESH
        )
    inside = []
    for step in OFFSETS:
        ok = jnp.logical_and(f + step >= 0, f + step < n)
        inside.append(ok)
        count = count + ok.astype(jnp.int32)

        @pl.when(ok)
        def _(step=step):
            pl.semaphore_signal(
                barrier, inc=1, device_id={"front": f + step}, device_id_type=MESH
            )
    pl.semaphore_wait(barrier, count)

    own_rows = rows(c * block, block)
    g_near = send(g_ref, gf.at[own_rows], col=ca)
    piece = block // 2
    g_far = [
        send(g_ref.at[pl.ds(k * piece, piece)], gf.at[rows(c * block + k * piece, piece)], col=cb)
        for k in range(2)
    ]

    l1_copy = send(l1.at[:, cols((1 - b0) * half, half)], l1f.at[rows(b0 * r1, r1)], front=fx)

    lines = lax.broadcasted_iota(jnp.int32, (sep, sep), 0)

    def chooser(row):
        return (lines == row).astype(F32).astype(BF)

    me1, me2, me3 = f % 2, f % 4, f % 8
    w1[me1, 0:r1] = i1[...]
    w1[me1, r1 : 2 * r1] = tmm(d_ref[...], chooser(map1[pl.ds(f // 2, 1), :])).astype(BF)
    in1 = rows(core * r1, r1)
    w1_copy = send(w1.at[me1, in1], w1.at[me1, in1], front=fx)
    w2[me2, 0:r2] = i2[...]
    w2[me2, r2 : 2 * r2] = tmm(e_ref[...], chooser(map2[pl.ds(f // 4, 1), :])).astype(BF)
    in2 = rows(core * r2, r2)
    w2_copies = [
        send(w2.at[me2, in2], w2.at[me2, in2], front=rotated(f, 4, k)) for k in (1, 2, 3)
    ]
    w3[me3] = i3[...]
    in3 = rows(core * (r3 // 2), r3 // 2)
    w3_copies = [
        send(w3.at[me3, in3], w3.at[me3, in3], front=rotated(f, 8, k)) for k in range(1, 8)
    ]
    l2_copies = [
        send(l2.at[:, quarter_of(rotated(f, 4, k))], l2f.at[rows(me2 * r2, r2)], front=rotated(f, 4, k))
        for k in (1, 2, 3)
    ]
    l3_copies = [
        send(l3.at[:, quarter_of(rotated(f, 8, k))], l3f.at[rows(me3 * r3, r3)], front=rotated(f, 8, k))
        for k in range(1, 8)
    ]
    gf[own_rows] = g_ref[...]
    l1f[rows(b0 * r1, r1)] = l1[:, cols(b0 * half, half)]
    l2f[rows(me2 * r2, r2)] = l2[:, quarter_of(f)]
    l3f[rows(me3 * r3, r3)] = l3[:, quarter_of(f)]
    for d in range(4):

        @pl.when(jnp.logical_not(inside[d ^ 1]))
        def _(d=d):
            got[d] = jnp.zeros(got.shape[1:], BF)

    ct[...] = tmm(c_ref[...], chooser(map0[...])).astype(BF)

    def leaf(slot, first=False):
        at = rows(slot * block, block)
        value = mm(gf[at], b_ref[...]).astype(BF)
        start[at] = value
        term = tmm(ct[at], value)
        part[...] = term if first else part[...] + term

    leaf(c, True)
    g_near.wait_recv()
    leaf(ca)
    g_pass = []
    for k in range(2):
        g_far[k].wait_recv()
        at = rows(cb * block + k * piece, piece)
        g_pass.append(send(gf.at[at], gf.at[at], col=ca))
    w1_copy.wait_recv()
    w1_pass = send(w1.at[1 - me1, in1], w1.at[1 - me1, in1], col=ca)
    leaf(cb)
    w2_pass = []
    for k in (1, 2, 3):
        w2_copies[k - 1].wait_recv()
        slot = (me2 + 4 - k) % 4
        w2_pass.append(send(w2.at[slot, in2], w2.at[slot, in2], col=ca))
    for k in range(2):
        g_pass[k].wait_recv()
    leaf(cd)

    def joined(w, at, size):
        return jnp.concatenate([w[m, at : at + size] for m in range(w.shape[0])], axis=0)

    give1[...] = part[:, cols((1 - b0) * half, half)].astype(BF)
    x1_copy = send(give1, x1, front=fx)
    w3_pass = []
    for k in range(1, 8):
        w3_copies[k - 1].wait_recv()
        slot = (me3 + 8 - k) % 8
        w3_pass.append(send(w3.at[slot, in3], w3.at[slot, in3], col=ca))
    l1_copy.wait_recv()
    w1_pass.wait_recv()
    x1_copy.wait_recv()
    rhs = l1f[...].astype(F32) - part[:, cols(b0 * half, half)] - x1[...].astype(F32)
    y1[...] = mm(joined(w1, 0, r1), rhs.astype(BF)).astype(BF)
    p2[...] = tmm(joined(w1, r1, r1), y1[...])
    give2[...] = p2[:, cols((1 - b1) * quarter, quarter)].astype(BF)
    x2_copy = send(give2, x2, front=fy)
    for copy in l2_copies + w2_pass:
        copy.wait_recv()
    x2_copy.wait_recv()
    rhs = l2f[...].astype(F32) - p2[:, cols(b1 * quarter, quarter)] - x2[...].astype(F32)
    y2[...] = mm(joined(w2, 0, r2), rhs.astype(BF)).astype(BF)
    term = tmm(joined(w2, r2, r2), y2[...])
    p3[...] = term.astype(BF)
    x3_copy = send(p3, x3, front=fz)
    for copy in l3_copies + w3_pass:
        copy.wait_recv()
    x3_copy.wait_recv()
    rhs = l3f[...].astype(F32) - p3[...].astype(F32) - x3[...].astype(F32)
    s3[...] = mm(joined(w3, 0, r3), rhs.astype(BF)).astype(BF)

    pull2 = mm(joined(w2, r2, r2), s3[...]).astype(BF)
    mine = cols(b1 * quarter, quarter)
    s2[:, mine] = (y2[...].astype(F32) - mm(joined(w2, 0, r2), pull2)).astype(BF)
    s2_copy = send(s2.at[:, mine], s2.at[:, mine], front=fy)
    o3_copies = []
    for k in (1, 2, 3):
        g = rotated(f, 4, k)
        o3_copies.append(send(s3.at[rows((g % 8) * r3, r3)], o3s.at[me2], front=g))
    o3s[me2] = s3[rows(me3 * r3, r3)]
    s2_copy.wait_recv()
    pull1 = mm(joined(w1, r1, r1), s2[...]).astype(BF)
    mine = cols(b0 * half, half)
    s1[:, mine] = (y1[...].astype(F32) - mm(joined(w1, 0, r1), pull1)).astype(BF)
    s1_copy = send(s1.at[:, mine], s1.at[:, mine], front=fx)
    o2_copy = send(s2.at[rows((fx % 4) * r2, r2)], o2s.at[me1], front=fx)
    o2s[me1] = s2[rows(me2 * r2, r2)]
    s1_copy.wait_recv()
    load_a.wait()
    chunk = block
    chunks = gf.shape[0] // chunk

    @pl.loop(0, chunks)
    def _(r):
        at = rows(r * chunk, chunk)
        pull[at] = mm(ct[at], s1[...]).astype(BF)

    @pl.loop(0, chunks)
    def _(r):
        at = rows(r * chunk, chunk)
        vol[at] = (start[at].astype(F32) - mm(gf[at], pull[...])).astype(BF)

    tile_chunks = got.shape[1] // chunk
    aimed = tile_ref[pl.ds(f, 1), :]
    aimed_a = jnp.broadcast_to(aimed[:, 0:1], (chunk, panel))
    aimed_b = jnp.broadcast_to(aimed[:, 1:2], (chunk, panel))

    def tile_copy(d, r):
        at = rows(r * chunk, chunk)
        return pltpu.make_async_remote_copy(
            src_ref=stage.at[d, at], dst_ref=got.at[d, at],
            send_sem=tile_send.at[d, r], recv_sem=tile_recv.at[d, r],
            device_id={"front": f + OFFSETS[d]}, device_id_type=MESH,
        )

    @pl.loop(0, tile_chunks)
    def _(r):
        at = rows(r * chunk, chunk)
        first = mm(av[1, at], vol[...])
        second = mm(av[2, at], vol[...])
        for d, step in enumerate(OFFSETS):
            goal = f + step
            stage[d, at] = jnp.where(
                aimed_a == goal, first, jnp.where(aimed_b == goal, second, 0.0)
            ).astype(BF)

            @pl.when(inside[d])
            def _(d=d):
                tile_copy(d, r).start()

    for copy in o3_copies + [o2_copy]:
        copy.wait_recv()
    o1[...] = s1[rows(me1 * r1, r1)]
    for m in range(2):
        o2[:, m * half : (m + 1) * half] = o2s[m]
    for m in range(4):
        at = (m % 2) * half + (m // 2) * quarter
        o3[:, at : at + quarter] = o3s[m]

    @pl.loop(0, tile_chunks)
    def _(r):
        at = rows(r * chunk, chunk)
        total = mm(av[0, at], vol[...])
        for d in range(4):
            back = d ^ 1

            @pl.when(inside[back])
            def _(d=d):
                tile_copy(d, r).wait_recv()

        for d in range(4):
            total = total + got[d, at].astype(F32)
        tiles[at] = total.astype(BF)

    for copy in copies:
        copy.wait_send()

    @pl.loop(0, tile_chunks)
    def _(r):
        for d in range(4):

            @pl.when(inside[d])
            def _(d=d):
                tile_copy(d, r).wait_send()


def local(
    leaf_load, leaf_inverse, leaf_coupling, leaf_rowmap,
    load_first, load_second, load_third,
    inverse_first, inverse_second, inverse_third,
    coupling_first, coupling_second, rowmap_first, rowmap_second,
    surface_coupling, neighbor_tiles,
):
    n = lax.axis_size("front")
    width = lax.axis_size("col")
    fr, panel = leaf_load.shape
    sep = leaf_coupling.shape[0]
    block = leaf_inverse.shape[0]
    tile = surface_coupling.shape[1]
    half, quarter = panel // 2, panel // 4
    r1, r2, r3 = inverse_first.shape[0], inverse_second.shape[0], inverse_third.shape[0]
    vmem = pl.BlockSpec(memory_space=pltpu.VMEM)

    def v(*shape, dtype=BF):
        return pltpu.VMEM(shape, dtype)

    return pl.pallas_call(
        functools.partial(kernel, n),
        out_shape=[
            jax.ShapeDtypeStruct(s, BF)
            for s in ((fr, panel), (tile, panel), (r1, panel), (r2, panel), (r3, panel))
        ],
        in_specs=[vmem] * 15 + [pl.BlockSpec(memory_space=pl.ANY)],
        out_specs=[vmem] * 5,
        scratch_shapes=[
            v(block * width, fr), v(fr, sep), v(fr, panel), v(sep, panel, dtype=F32),
            v(2, 2 * r1, sep), v(4, 2 * r2, sep), v(8, r3, sep),
            v(sep, half), v(sep, quarter), v(sep, quarter),
            v(sep, half), v(sep, half), v(sep, half), v(sep, half, dtype=F32),
            v(sep, quarter), v(sep, quarter), v(sep, quarter), v(sep, quarter), v(sep, quarter),
            v(sep, quarter), v(sep, half), v(sep, panel),
            v(4, r3, quarter), v(2, r2, half), v(fr, panel),
            v(*surface_coupling.shape), v(4, tile, panel), v(4, tile, panel),
            pltpu.SemaphoreType.DMA((64,)), pltpu.SemaphoreType.DMA((64,)),
            pltpu.SemaphoreType.DMA((4, tile // block)), pltpu.SemaphoreType.DMA((4, tile // block)),
            pltpu.SemaphoreType.DMA,
        ],
        compiler_params=pltpu.CompilerParams(
            collective_id=0, has_side_effects=True, vmem_limit_bytes=56 * 1024 * 1024
        ),
        cost_estimate=pl.CostEstimate(
            flops=12 * fr * fr * panel, bytes_accessed=16 * fr * fr, transcendentals=0
        ),
    )(
        leaf_load, leaf_inverse, leaf_coupling, leaf_rowmap,
        load_first, load_second, load_third,
        inverse_first, inverse_second, inverse_third,
        coupling_first, coupling_second, rowmap_first, rowmap_second, neighbor_tiles,
        surface_coupling,
    )


def solution(mesh):
    return jax.shard_map(
        local,
        mesh=mesh,
        in_specs=(
            P("front", "col"), P(("front", "col"), None), P("front", None), P("front", None),
            P("front", "col"), P("front", "col"), P("front", "col"),
            P("front", None), P("front", None), P("front", None),
            P(None, "front"), P(None, "front"), P(), P(),
            P("front", None, None), P(),
        ),
        out_specs=(P("front", "col"),) * 5,
        check_vma=False,
    )
```

```python
import functools

import jax
import jax.numpy as jnp
from jax import lax
from jax.experimental import pallas as pl
from jax.experimental.pallas import tpu as pltpu
from jax.sharding import PartitionSpec as P

BF = jnp.bfloat16
F32 = jnp.float32
MESH = pl.DeviceIdType.MESH
X, Z_ON, Z_BACK, DIAGONAL = range(4)


def mm(a, b):
    return jnp.dot(a, b, preferred_element_type=F32)


def tmm(a, b):
    return lax.dot_general(a, b, (((0,), (0,)), ((), ())), preferred_element_type=F32)


def flip(x, bit):
    return x + bit * (1 - 2 * ((x // bit) % 2))


def rotated(x, size, step):
    return (x // size) * size + (x % size + step) % size


def kernel(
    n, b_ref, g_ref, c_ref, map0, l1, l2, l3, i1, i2, i3, d_ref, e_ref, map1, map2, tile_ref, a_hbm,
    vol, tiles, o1, o2, o3,
    gf, ct, start, part, w1, w2, w3, l1f, l2f, l3f,
    give1, x1, y1, p2, x2, y2, p3, x3, s3, s2, s1, o3s, o2s, pull, value, av, stage, got, bent,
    send_sem, recv_sem, tile_send, tile_recv, a_sem,
):
    f = lax.axis_index("front")
    c = lax.axis_index("col")
    core = c % 2
    ca, cb = flip(c, 1), flip(c, 2)
    cd = flip(ca, 2)
    b0, b1 = f % 2, (f // 2) % 2
    fx, fy, fz = flip(f, 1), flip(f, 2), flip(f, 4)
    sep = l1f.shape[0]
    panel = b_ref.shape[1]
    half, quarter = panel // 2, panel // 4
    block = g_ref.shape[0]
    r1, r2, r3 = i1.shape[0], i2.shape[0], i3.shape[0]

    def cols(at, size):
        return pl.ds(pl.multiple_of(at, 128), size)

    def rows(at, size):
        return pl.ds(pl.multiple_of(at, 16), size)

    def half_of(g):
        return cols((g % 2) * half, half)

    copies = []

    def send(src, dst, **where):
        i = len(copies)
        copy = pltpu.make_async_remote_copy(
            src_ref=src, dst_ref=dst, send_sem=send_sem.at[i], recv_sem=recv_sem.at[i],
            device_id=where, device_id_type=MESH,
        )
        copies.append(copy)
        copy.start()
        return copy

    load_a = pltpu.make_async_copy(a_hbm, av, a_sem)
    load_a.start()

    barrier = pltpu.get_barrier_semaphore()
    for other in (ca, cb):
        pl.semaphore_signal(barrier, inc=1, device_id={"col": other}, device_id_type=MESH)
    for k in range(1, 8):
        pl.semaphore_signal(
            barrier, inc=1, device_id={"front": rotated(f, 8, k)}, device_id_type=MESH
        )
    ahead = f + 2 * (2 * b0 - 1)
    behind = f - 2 * (2 * b0 - 1)
    has_ahead = jnp.logical_and(ahead >= 0, ahead < n)
    has_behind = jnp.logical_and(behind >= 0, behind < n)
    for ok, other in ((has_ahead, ahead), (has_behind, behind)):

        @pl.when(ok)
        def _(other=other):
            pl.semaphore_signal(barrier, inc=1, device_id={"front": other}, device_id_type=MESH)
    count = 9 + has_ahead.astype(jnp.int32) + has_behind.astype(jnp.int32)
    pl.semaphore_wait(barrier, count)

    own_rows = rows(c * block, block)
    g_near = send(g_ref, gf.at[own_rows], col=ca)
    piece = block // 2
    g_far = [
        send(g_ref.at[pl.ds(k * piece, piece)], gf.at[rows(c * block + k * piece, piece)], col=cb)
        for k in range(2)
    ]

    l1_copy = send(l1.at[:, cols((1 - b0) * half, half)], l1f.at[rows(b0 * r1, r1)], front=fx)

    lines = lax.broadcasted_iota(jnp.int32, (sep, sep), 0)

    def chooser(row):
        return (lines == row).astype(F32).astype(BF)

    me1, me2, me3 = f % 2, f % 4, f % 8
    w1[me1, 0:r1] = i1[...]
    w1[me1, r1 : 2 * r1] = tmm(d_ref[...], chooser(map1[pl.ds(f // 2, 1), :])).astype(BF)
    in1 = rows(core * r1, r1)
    w1_copy = send(w1.at[me1, in1], w1.at[me1, in1], front=fx)
    w2[me2, 0:r2] = i2[...]
    w2[me2, r2 : 2 * r2] = tmm(e_ref[...], chooser(map2[pl.ds(f // 4, 1), :])).astype(BF)
    in2 = rows(core * r2, r2)
    w2_copies = [
        send(w2.at[me2, in2], w2.at[me2, in2], front=rotated(f, 4, k)) for k in (1, 2, 3)
    ]
    w3[me3] = i3[...]
    in3 = rows(core * (r3 // 2), r3 // 2)
    w3_copies = [
        send(w3.at[me3, in3], w3.at[me3, in3], front=rotated(f, 8, k)) for k in range(1, 8)
    ]
    l2_copies = [
        send(l2.at[:, half_of(rotated(f, 4, k))], l2f.at[rows(me2 * r2, r2)], front=rotated(f, 4, k))
        for k in (1, 2, 3)
    ]
    l3_copies = [
        send(l3.at[:, half_of(rotated(f, 8, k))], l3f.at[rows(me3 * r3, r3)], front=rotated(f, 8, k))
        for k in range(1, 8)
    ]
    gf[own_rows] = g_ref[...]
    l1f[rows(b0 * r1, r1)] = l1[:, cols(b0 * half, half)]
    l2f[rows(me2 * r2, r2)] = l2[:, half_of(f)]
    l3f[rows(me3 * r3, r3)] = l3[:, half_of(f)]

    @pl.when(jnp.logical_not(has_behind))
    def _():
        got[:, Z_ON] = jnp.zeros((2,) + got.shape[2:], BF)
        bent[...] = jnp.zeros(bent.shape, BF)

    @pl.when(jnp.logical_not(has_ahead))
    def _():
        got[:, Z_BACK] = jnp.zeros((2,) + got.shape[2:], BF)

    ct[...] = tmm(c_ref[...], chooser(map0[...])).astype(BF)

    def leaf(slot, first=False):
        at = rows(slot * block, block)
        solved = mm(gf[at], b_ref[...]).astype(BF)
        start[at] = solved
        term = tmm(ct[at], solved)
        part[...] = term if first else part[...] + term

    leaf(c, True)
    g_near.wait_recv()
    leaf(ca)
    g_pass = []
    for k in range(2):
        g_far[k].wait_recv()
        at = rows(cb * block + k * piece, piece)
        g_pass.append(send(gf.at[at], gf.at[at], col=ca))
    w1_copy.wait_recv()
    w1_pass = send(w1.at[1 - me1, in1], w1.at[1 - me1, in1], col=ca)
    leaf(cb)
    w2_pass = []
    for k in (1, 2, 3):
        w2_copies[k - 1].wait_recv()
        slot = (me2 + 4 - k) % 4
        w2_pass.append(send(w2.at[slot, in2], w2.at[slot, in2], col=ca))
    for k in range(2):
        g_pass[k].wait_recv()
    leaf(cd)

    def joined(w, at, size):
        return jnp.concatenate([w[m, at : at + size] for m in range(w.shape[0])], axis=0)

    def in_half(k):
        return pl.ds(k * quarter, quarter)

    def in_panel(which, k):
        return cols(which * half + k * quarter, quarter)

    x1_copies = []
    for k in range(2):
        give1[k] = part[:, in_panel(1 - b0, k)].astype(BF)
        x1_copies.append(send(give1.at[k], x1.at[k], front=fx))
    w3_pass = []
    for k in range(1, 8):
        w3_copies[k - 1].wait_recv()
        slot = (me3 + 8 - k) % 8
        w3_pass.append(send(w3.at[slot, in3], w3.at[slot, in3], col=ca))
    l1_copy.wait_recv()
    w1_pass.wait_recv()
    x2_copies = []
    for k in range(2):
        x1_copies[k].wait_recv()
        rhs = l1f[:, in_half(k)].astype(F32) - part[:, in_panel(b0, k)] - x1[k].astype(F32)
        y1[k] = mm(joined(w1, 0, r1), rhs.astype(BF)).astype(BF)
        p2[k] = tmm(joined(w1, r1, r1), y1[k]).astype(BF)
        x2_copies.append(send(p2.at[k], x2.at[k], front=fy))
    for copy in l2_copies + w2_pass:
        copy.wait_recv()
    x3_copies = []
    for k in range(2):
        x2_copies[k].wait_recv()
        rhs = l2f[:, in_half(k)].astype(F32) - p2[k].astype(F32) - x2[k].astype(F32)
        y2[k] = mm(joined(w2, 0, r2), rhs.astype(BF)).astype(BF)
        p3[k] = tmm(joined(w2, r2, r2), y2[k]).astype(BF)
        x3_copies.append(send(p3.at[k], x3.at[k], front=fz))
    for copy in l3_copies + w3_pass:
        copy.wait_recv()

    s1_copies = []
    for k in range(2):
        x3_copies[k].wait_recv()
        rhs = l3f[:, in_half(k)].astype(F32) - p3[k].astype(F32) - x3[k].astype(F32)
        top = mm(joined(w3, 0, r3), rhs.astype(BF)).astype(BF)
        s3[:, in_half(k)] = top
        pull2 = mm(joined(w2, r2, r2), top).astype(BF)
        second = (y2[k].astype(F32) - mm(joined(w2, 0, r2), pull2)).astype(BF)
        s2[:, in_half(k)] = second
        pull1 = mm(joined(w1, r1, r1), second).astype(BF)
        s1[k, b0] = (y1[k].astype(F32) - mm(joined(w1, 0, r1), pull1)).astype(BF)
        s1_copies.append(send(s1.at[k, b0], s1.at[k, b0], front=fx))
    o3_copy = send(s3.at[rows((fx % 8) * r3, r3)], o3s.at[b0], front=fx)
    o2_copy = send(s2.at[rows((fx % 4) * r2, r2)], o2s.at[b0], front=fx)
    load_a.wait()

    chunk = block
    chunks = gf.shape[0] // chunk
    tile_chunks = got.shape[2] // chunk
    aimed = jnp.sum(
        jnp.where(
            lax.broadcasted_iota(jnp.int32, tile_ref.shape, 1) == f,
            tile_ref[...].astype(F32), 0.0,
        ),
        axis=1, keepdims=True,
    )
    aimed_a = jnp.broadcast_to(aimed[0:1], (chunk, half))
    aimed_b = jnp.broadcast_to(aimed[1:2], (chunk, half))
    goals = (fx, ahead, behind, fx + ahead - f)

    def tile_copy(k, kind, r, parity):
        at = rows(r * chunk, chunk)
        if kind == DIAGONAL:
            target, landing = (fx if parity else ahead), bent.at[k, at]
        else:
            target, landing = goals[kind], got.at[k, kind, at]
        return pltpu.make_async_remote_copy(
            src_ref=stage.at[k, kind, at], dst_ref=landing,
            send_sem=tile_send.at[k, kind, r], recv_sem=tile_recv.at[k, kind, r],
            device_id={"front": target}, device_id_type=MESH,
        )

    def volume(k):
        s1_copies[k].wait_recv()
        both = jnp.concatenate([s1[k, 0], s1[k, 1]], axis=1)

        @pl.loop(0, chunks)
        def _(r):
            at = rows(r * chunk, chunk)
            pull[at] = mm(ct[at], both).astype(BF)

        @pl.loop(0, chunks)
        def _(r):
            at = rows(r * chunk, chunk)
            change = mm(gf[at], pull[...])
            for m in range(2):
                here = pl.ds(m * half + k * quarter, quarter)
                new = (
                    start[at, here].astype(F32) - change[:, m * quarter : (m + 1) * quarter]
                ).astype(BF)
                vol[at, here] = new
                value[k, at, pl.ds(m * quarter, quarter)] = new

    def contribute(k):
        @pl.loop(0, tile_chunks // 2)
        def _(pair):
            for parity in range(2):
                r = pair * 2 + parity
                at = rows(r * chunk, chunk)
                first = mm(av[1, at], value[k])
                second = mm(av[2, at], value[k])
                for kind in (DIAGONAL, X, Z_ON, Z_BACK):
                    goal = goals[kind].astype(F32)
                    stage[k, kind, at] = jnp.where(
                        aimed_a == goal, first, jnp.where(aimed_b == goal, second, 0.0)
                    ).astype(BF)

                @pl.when(has_ahead)
                def _():
                    tile_copy(k, DIAGONAL, r, parity).start()
                    tile_copy(k, Z_ON, r, parity).start()

                if parity:
                    tile_copy(k, X, r, parity).start()
                else:

                    @pl.when(has_behind)
                    def _():
                        tile_copy(k, Z_BACK, r, parity).start()

    def bend(k):
        @pl.loop(0, tile_chunks // 2)
        def _(pair):
            for parity in range(2):
                r = pair * 2 + parity
                at = rows(r * chunk, chunk)
                kind = Z_BACK if parity else X

                @pl.when(has_behind)
                def _():
                    tile_copy(k, DIAGONAL, r, parity).wait_recv()

                stage[k, kind, at] = (
                    stage[k, kind, at].astype(F32) + bent[k, at].astype(F32)
                ).astype(BF)
                if parity:

                    @pl.when(has_behind)
                    def _():
                        tile_copy(k, Z_BACK, r, parity).start()
                else:
                    tile_copy(k, X, r, parity).start()

    def collect(k):
        @pl.loop(0, tile_chunks)
        def _(r):
            at = rows(r * chunk, chunk)
            total = mm(av[0, at], value[k])
            tile_copy(k, X, r, 0).wait_recv()

            @pl.when(has_behind)
            def _():
                tile_copy(k, Z_ON, r, 0).wait_recv()

            @pl.when(has_ahead)
            def _():
                tile_copy(k, Z_BACK, r, 0).wait_recv()

            for kind in (X, Z_ON, Z_BACK):
                total = total + got[k, kind, at].astype(F32)
            for m in range(2):
                tiles[at, pl.ds(m * half + k * quarter, quarter)] = total[
                    :, m * quarter : (m + 1) * quarter
                ].astype(BF)

    volume(0)
    contribute(0)
    volume(1)
    bend(0)
    contribute(1)

    o3s[b0] = s3[rows(me3 * r3, r3)]
    o2s[b0] = s2[rows(me2 * r2, r2)]
    for k in range(2):
        for m in range(2):
            o1[:, m * half + k * quarter : m * half + (k + 1) * quarter] = s1[
                k, m, rows(me1 * r1, r1)
            ]
    o2_copy.wait_recv()
    o3_copy.wait_recv()
    for m in range(2):
        o2[:, m * half : (m + 1) * half] = o2s[m]
        o3[:, m * half : (m + 1) * half] = o3s[m]

    bend(1)
    collect(0)
    collect(1)

    for copy in copies:
        copy.wait_send()
    for k in range(2):

        @pl.loop(0, tile_chunks)
        def _(r):
            tile_copy(k, X, r, 0).wait_send()

            @pl.when(has_ahead)
            def _():
                tile_copy(k, Z_ON, r, 0).wait_send()
                tile_copy(k, DIAGONAL, r, 0).wait_send()

            @pl.when(has_behind)
            def _():
                tile_copy(k, Z_BACK, r, 0).wait_send()


def hand_over(*refs):
    sems = refs[-1]
    count = (len(refs) - 1) // 2
    copies = [
        pltpu.make_async_copy(refs[i], refs[count + i], sems.at[i]) for i in range(count)
    ]
    for copy in copies:
        copy.start()
    for copy in copies:
        copy.wait()


def local(
    leaf_load, leaf_inverse, leaf_coupling, leaf_rowmap,
    load_first, load_second, load_third,
    inverse_first, inverse_second, inverse_third,
    coupling_first, coupling_second, rowmap_first, rowmap_second,
    surface_coupling, neighbor_tiles,
):
    n = lax.axis_size("front")
    width = lax.axis_size("col")
    fr, panel = leaf_load.shape
    sep = leaf_coupling.shape[0]
    block = leaf_inverse.shape[0]
    tile = surface_coupling.shape[1]
    half, quarter = panel // 2, panel // 4
    r1, r2, r3 = inverse_first.shape[0], inverse_second.shape[0], inverse_third.shape[0]
    vmem = pl.BlockSpec(memory_space=pltpu.VMEM)

    def v(*shape, dtype=BF):
        return pltpu.VMEM(shape, dtype)

    results = pl.pallas_call(
        functools.partial(kernel, n),
        out_shape=[
            jax.ShapeDtypeStruct(s, BF)
            for s in ((fr, panel), (tile, panel), (r1, panel), (r2, panel), (r3, panel))
        ],
        in_specs=[vmem] * 15 + [pl.BlockSpec(memory_space=pl.ANY)],
        out_specs=[vmem] * 5,
        scratch_shapes=[
            v(block * width, fr), v(fr, sep), v(fr, panel), v(sep, panel, dtype=F32),
            v(2, 2 * r1, sep), v(4, 2 * r2, sep), v(8, r3, sep),
            v(sep, half), v(sep, half), v(sep, half),
            v(2, sep, quarter), v(2, sep, quarter), v(2, sep, quarter), v(2, sep, quarter),
            v(2, sep, quarter), v(2, sep, quarter), v(2, sep, quarter), v(2, sep, quarter),
            v(sep, half), v(sep, half), v(2, 2, sep, quarter),
            v(2, r3, half), v(2, r2, half), v(fr, half), v(2, fr, half),
            v(*surface_coupling.shape), v(2, 4, tile, half), v(2, 3, tile, half), v(2, tile, half),
            pltpu.SemaphoreType.DMA((64,)), pltpu.SemaphoreType.DMA((64,)),
            pltpu.SemaphoreType.DMA((2, 4, tile // block)),
            pltpu.SemaphoreType.DMA((2, 4, tile // block)),
            pltpu.SemaphoreType.DMA,
        ],
        compiler_params=pltpu.CompilerParams(
            collective_id=0, has_side_effects=True, vmem_limit_bytes=56 * 1024 * 1024
        ),
        cost_estimate=pl.CostEstimate(
            flops=12 * fr * fr * panel, bytes_accessed=16 * fr * fr, transcendentals=0
        ),
    )(
        leaf_load, leaf_inverse, leaf_coupling, leaf_rowmap,
        load_first, load_second, load_third,
        inverse_first, inverse_second, inverse_third,
        coupling_first, coupling_second, rowmap_first, rowmap_second, neighbor_tiles.T,
        surface_coupling,
    )
    hbm = pl.BlockSpec(memory_space=pl.ANY)
    return pl.pallas_call(
        hand_over,
        out_shape=[jax.ShapeDtypeStruct(x.shape, x.dtype) for x in results],
        in_specs=[hbm] * 5,
        out_specs=[hbm] * 5,
        scratch_shapes=[pltpu.SemaphoreType.DMA((5,))],
        compiler_params=pltpu.CompilerParams(vmem_limit_bytes=60 * 1024 * 1024),
    )(*results)


def solution(mesh):
    return jax.shard_map(
        local,
        mesh=mesh,
        in_specs=(
            P("front", "col"), P(("front", "col"), None), P("front", None), P("front", None),
            P("front", "col"), P("front", "col"), P("front", "col"),
            P("front", None), P("front", None), P("front", None),
            P(None, "front"), P(None, "front"), P(), P(),
            P("front", None, None), P(),
        ),
        out_specs=(P("front", "col"),) * 5,
        check_vma=False,
    )
```

```python
import functools

import jax
import jax.numpy as jnp
from jax import lax
from jax.experimental import pallas as pl
from jax.experimental.pallas import tpu as pltpu
from jax.sharding import PartitionSpec as P

BF = jnp.bfloat16
F32 = jnp.float32
MESH = pl.DeviceIdType.MESH
X, Z_ON, Z_BACK, DIAGONAL = range(4)


def mm(a, b):
    return jnp.dot(a, b, preferred_element_type=F32)


def tmm(a, b):
    return lax.dot_general(a, b, (((0,), (0,)), ((), ())), preferred_element_type=F32)


def flip(x, bit):
    return x + bit * (1 - 2 * ((x // bit) % 2))


def kernel(
    n, b_hbm, g_ref, c_hbm, map0, l1, l2, l3, i1, i2, i3, d_ref, e_ref, map1, map2, tile_ref, a_hbm,
    vol, tiles, o1, o2, o3,
    gf, ct, start, part, w1, w2, w3, l1f, l2f, l3f,
    b_ref, c_ref, give1, x1, y1, p2, x2, y2, p3, x3, s3, s2, s1, o3s, o2s, pull, value, av, stage, got, bent,
    send_sem, recv_sem, tile_send, tile_recv, load_sem,
):
    f = lax.axis_index("front")
    c = lax.axis_index("col")
    core = c % 2
    ca, cb = flip(c, 1), flip(c, 2)
    cd = flip(ca, 2)
    b0, b1 = f % 2, (f // 2) % 2
    fx, fy, fz = flip(f, 1), flip(f, 2), flip(f, 4)
    sep = l1f.shape[0]
    panel = b_ref.shape[1]
    half, quarter = panel // 2, panel // 4
    block = g_ref.shape[0]
    r1, r2, r3 = i1.shape[0], i2.shape[0], i3.shape[0]

    def cols(at, size):
        return pl.ds(pl.multiple_of(at, 128), size)

    def rows(at, size):
        return pl.ds(pl.multiple_of(at, 16), size)

    def half_of(g):
        return cols((g % 2) * half, half)

    copies = []

    def send(src, dst, **where):
        i = len(copies)
        copy = pltpu.make_async_remote_copy(
            src_ref=src, dst_ref=dst, send_sem=send_sem.at[i], recv_sem=recv_sem.at[i],
            device_id=where, device_id_type=MESH,
        )
        copies.append(copy)
        copy.start()
        return copy

    loads = [
        pltpu.make_async_copy(src, dst, load_sem.at[i])
        for i, (src, dst) in enumerate(((b_hbm, b_ref), (c_hbm, c_ref), (a_hbm, av)))
    ]
    for load in loads:
        load.start()

    barrier = pltpu.get_barrier_semaphore()
    for other in (ca, cb):
        pl.semaphore_signal(barrier, inc=1, device_id={"col": other}, device_id_type=MESH)
    for other in (fx, fy, fz):
        pl.semaphore_signal(barrier, inc=1, device_id={"front": other}, device_id_type=MESH)
    ahead = f + 2 * (2 * b0 - 1)
    behind = f - 2 * (2 * b0 - 1)
    has_ahead = jnp.logical_and(ahead >= 0, ahead < n)
    has_behind = jnp.logical_and(behind >= 0, behind < n)
    for ok, other in ((has_ahead, ahead), (has_behind, behind)):

        @pl.when(ok)
        def _(other=other):
            pl.semaphore_signal(barrier, inc=1, device_id={"front": other}, device_id_type=MESH)
    count = 5 + has_ahead.astype(jnp.int32) + has_behind.astype(jnp.int32)
    pl.semaphore_wait(barrier, count)

    own_rows = rows(c * block, block)
    g_near = send(g_ref, gf.at[own_rows], col=ca)
    piece = block // 2
    g_far = [
        send(g_ref.at[pl.ds(k * piece, piece)], gf.at[rows(c * block + k * piece, piece)], col=cb)
        for k in range(2)
    ]

    lines = lax.broadcasted_iota(jnp.int32, (sep, sep), 0)

    def chooser(row):
        return (lines == row).astype(F32).astype(BF)

    me1, me2, me3 = f % 2, f % 4, f % 8
    pair2, pair3, four3 = me2 - b0, me3 - b0, (me3 // 4) * 4
    in1, in2, in3 = rows(core * r1, r1), rows(core * r2, r2), rows(core * (r3 // 2), r3 // 2)
    w2[me2, 0:r2] = i2[...]
    w2[me2, r2 : 2 * r2] = tmm(e_ref[...], chooser(map2[pl.ds(f // 4, 1), :])).astype(BF)
    w3[me3] = i3[...]
    w2_x = send(w2.at[me2, in2], w2.at[me2, in2], front=fx)
    l2_x = send(l2.at[:, half_of(fx)], l2f.at[rows(me2 * r2, r2)], front=fx)
    w3_x = send(w3.at[me3, in3], w3.at[me3, in3], front=fx)
    l3_x = send(l3.at[:, half_of(fx)], l3f.at[rows(me3 * r3, r3)], front=fx)
    w1[me1, 0:r1] = i1[...]
    w1[me1, r1 : 2 * r1] = tmm(d_ref[...], chooser(map1[pl.ds(f // 2, 1), :])).astype(BF)
    w1_copy = send(w1.at[me1, in1], w1.at[me1, in1], front=fx)
    l1_copy = send(l1.at[:, half_of(fx)], l1f.at[rows(b0 * r1, r1)], front=fx)
    gf[own_rows] = g_ref[...]
    l1f[rows(b0 * r1, r1)] = l1[:, half_of(f)]
    l2f[rows(me2 * r2, r2)] = l2[:, half_of(f)]
    l3f[rows(me3 * r3, r3)] = l3[:, half_of(f)]

    @pl.when(jnp.logical_not(has_behind))
    def _():
        got[:, Z_ON] = jnp.zeros((2,) + got.shape[2:], BF)
        bent[...] = jnp.zeros(bent.shape, BF)

    @pl.when(jnp.logical_not(has_ahead))
    def _():
        got[:, Z_BACK] = jnp.zeros((2,) + got.shape[2:], BF)

    loads[1].wait()
    ct[...] = tmm(c_ref[...], chooser(map0[...])).astype(BF)

    def leaf(slot, first=False):
        at = rows(slot * block, block)
        solved = mm(gf[at], b_ref[...]).astype(BF)
        start[at] = solved
        term = tmm(ct[at], solved)
        part[...] = term if first else part[...] + term

    loads[0].wait()
    leaf(c, True)
    g_near.wait_recv()
    leaf(ca)
    for copy in (w2_x, l2_x, w3_x, l3_x):
        copy.wait_recv()
    two = w2.at[pl.ds(pair2, 2), in2]
    w2_y = send(two, two, front=fy)
    two = l2f.at[rows(pair2 * r2, 2 * r2)]
    l2_y = send(two, two, front=fy)
    two = w3.at[pl.ds(pair3, 2), in3]
    w3_y = send(two, two, front=fy)
    two = l3f.at[rows(pair3 * r3, 2 * r3)]
    l3_y = send(two, two, front=fy)
    g_pass = []
    for k in range(2):
        g_far[k].wait_recv()
        at = rows(cb * block + k * piece, piece)
        g_pass.append(send(gf.at[at], gf.at[at], col=ca))
    one = w2.at[flip(me2, 1), in2]
    w2_pass = [send(one, one, col=ca)]
    one = w3.at[flip(me3, 1), in3]
    w3_pass = [send(one, one, col=ca)]
    leaf(cb)
    w1_copy.wait_recv()
    one = w1.at[1 - me1, in1]
    w1_pass = send(one, one, col=ca)
    for k in range(2):
        g_pass[k].wait_recv()
    leaf(cd)

    def joined(w, at, size):
        return jnp.concatenate([w[m, at : at + size] for m in range(w.shape[0])], axis=0)

    def in_half(k):
        return pl.ds(k * quarter, quarter)

    def in_panel(which, k):
        return cols(which * half + k * quarter, quarter)

    x1_copies = []
    for k in range(2):
        give1[k] = part[:, in_panel(1 - b0, k)].astype(BF)
        x1_copies.append(send(give1.at[k], x1.at[k], front=fx))
    for copy in (w2_y, w3_y, l3_y):
        copy.wait_recv()
    four = w3.at[pl.ds(four3, 4), in3]
    w3_z = send(four, four, front=fz)
    four = l3f.at[rows(four3 * r3, 4 * r3)]
    l3_z = send(four, four, front=fz)
    two = w2.at[pl.ds(2 - pair2, 2), in2]
    w2_pass.append(send(two, two, col=ca))
    two = w3.at[pl.ds(four3 + 2 - (pair3 - four3), 2), in3]
    w3_pass.append(send(two, two, col=ca))
    l1_copy.wait_recv()
    w1_pass.wait_recv()
    x2_copies = []
    for k in range(2):
        x1_copies[k].wait_recv()
        rhs = l1f[:, in_half(k)].astype(F32) - part[:, in_panel(b0, k)] - x1[k].astype(F32)
        y1[k] = mm(joined(w1, 0, r1), rhs.astype(BF)).astype(BF)
        p2[k] = tmm(joined(w1, r1, r1), y1[k]).astype(BF)
        x2_copies.append(send(p2.at[k], x2.at[k], front=fy))
    for copy in [l2_y] + w2_pass:
        copy.wait_recv()
    x3_copies = []
    for k in range(2):
        x2_copies[k].wait_recv()
        rhs = l2f[:, in_half(k)].astype(F32) - p2[k].astype(F32) - x2[k].astype(F32)
        y2[k] = mm(joined(w2, 0, r2), rhs.astype(BF)).astype(BF)
        p3[k] = tmm(joined(w2, r2, r2), y2[k]).astype(BF)
        x3_copies.append(send(p3.at[k], x3.at[k], front=fz))
    w3_z.wait_recv()
    four = w3.at[pl.ds(4 - four3, 4), in3]
    w3_pass.append(send(four, four, col=ca))
    for copy in [l3_z] + w3_pass:
        copy.wait_recv()

    s1_copies = []
    for k in range(2):
        x3_copies[k].wait_recv()
        rhs = l3f[:, in_half(k)].astype(F32) - p3[k].astype(F32) - x3[k].astype(F32)
        top = mm(joined(w3, 0, r3), rhs.astype(BF)).astype(BF)
        s3[:, in_half(k)] = top
        pull2 = mm(joined(w2, r2, r2), top).astype(BF)
        second = (y2[k].astype(F32) - mm(joined(w2, 0, r2), pull2)).astype(BF)
        s2[:, in_half(k)] = second
        pull1 = mm(joined(w1, r1, r1), second).astype(BF)
        s1[k, b0] = (y1[k].astype(F32) - mm(joined(w1, 0, r1), pull1)).astype(BF)
        s1_copies.append(send(s1.at[k, b0], s1.at[k, b0], front=fx))
    o3_copy = send(s3.at[rows((fx % 8) * r3, r3)], o3s.at[b0], front=fx)
    o2_copy = send(s2.at[rows((fx % 4) * r2, r2)], o2s.at[b0], front=fx)
    loads[2].wait()

    chunk = block
    chunks = gf.shape[0] // chunk
    tile_chunks = got.shape[2] // chunk
    aimed = jnp.sum(
        jnp.where(
            lax.broadcasted_iota(jnp.int32, tile_ref.shape, 1) == f,
            tile_ref[...].astype(F32), 0.0,
        ),
        axis=1, keepdims=True,
    )
    aimed_a = jnp.broadcast_to(aimed[0:1], (chunk, half))
    aimed_b = jnp.broadcast_to(aimed[1:2], (chunk, half))
    goals = (fx, ahead, behind, fx + ahead - f)

    def tile_copy(k, kind, r, parity):
        at = rows(r * chunk, chunk)
        if kind == DIAGONAL:
            target, landing = (fx if parity else ahead), bent.at[k, at]
        else:
            target, landing = goals[kind], got.at[k, kind, at]
        return pltpu.make_async_remote_copy(
            src_ref=stage.at[k, kind, at], dst_ref=landing,
            send_sem=tile_send.at[k, kind, r], recv_sem=tile_recv.at[k, kind, r],
            device_id={"front": target}, device_id_type=MESH,
        )

    def volume(k):
        s1_copies[k].wait_recv()
        both = jnp.concatenate([s1[k, 0], s1[k, 1]], axis=1)

        @pl.loop(0, chunks)
        def _(r):
            at = rows(r * chunk, chunk)
            pull[at] = mm(ct[at], both).astype(BF)

        @pl.loop(0, chunks)
        def _(r):
            at = rows(r * chunk, chunk)
            change = mm(gf[at], pull[...])
            for m in range(2):
                here = pl.ds(m * half + k * quarter, quarter)
                new = (
                    start[at, here].astype(F32) - change[:, m * quarter : (m + 1) * quarter]
                ).astype(BF)
                vol[at, here] = new
                value[k, at, pl.ds(m * quarter, quarter)] = new

    def contribute(k):
        @pl.loop(0, tile_chunks // 2)
        def _(pair):
            for parity in range(2):
                r = pair * 2 + parity
                at = rows(r * chunk, chunk)
                first = mm(av[1, at], value[k])
                second = mm(av[2, at], value[k])
                for kind in (DIAGONAL, X, Z_ON, Z_BACK):
                    goal = goals[kind].astype(F32)
                    stage[k, kind, at] = jnp.where(
                        aimed_a == goal, first, jnp.where(aimed_b == goal, second, 0.0)
                    ).astype(BF)

                @pl.when(has_ahead)
                def _():
                    tile_copy(k, DIAGONAL, r, parity).start()
                    tile_copy(k, Z_ON, r, parity).start()

                if parity:
                    tile_copy(k, X, r, parity).start()
                else:

                    @pl.when(has_behind)
                    def _():
                        tile_copy(k, Z_BACK, r, parity).start()

    def bend(k):
        @pl.loop(0, tile_chunks // 2)
        def _(pair):
            for parity in range(2):
                r = pair * 2 + parity
                at = rows(r * chunk, chunk)
                kind = Z_BACK if parity else X

                @pl.when(has_behind)
                def _():
                    tile_copy(k, DIAGONAL, r, parity).wait_recv()

                stage[k, kind, at] = (
                    stage[k, kind, at].astype(F32) + bent[k, at].astype(F32)
                ).astype(BF)
                if parity:

                    @pl.when(has_behind)
                    def _():
                        tile_copy(k, Z_BACK, r, parity).start()
                else:
                    tile_copy(k, X, r, parity).start()

    def collect(k):
        @pl.loop(0, tile_chunks)
        def _(r):
            at = rows(r * chunk, chunk)
            total = mm(av[0, at], value[k])
            tile_copy(k, X, r, 0).wait_recv()

            @pl.when(has_behind)
            def _():
                tile_copy(k, Z_ON, r, 0).wait_recv()

            @pl.when(has_ahead)
            def _():
                tile_copy(k, Z_BACK, r, 0).wait_recv()

            for kind in (X, Z_ON, Z_BACK):
                total = total + got[k, kind, at].astype(F32)
            for m in range(2):
                tiles[at, pl.ds(m * half + k * quarter, quarter)] = total[
                    :, m * quarter : (m + 1) * quarter
                ].astype(BF)

    volume(0)
    contribute(0)
    volume(1)
    bend(0)
    contribute(1)

    o3s[b0] = s3[rows(me3 * r3, r3)]
    o2s[b0] = s2[rows(me2 * r2, r2)]
    for k in range(2):
        for m in range(2):
            o1[:, m * half + k * quarter : m * half + (k + 1) * quarter] = s1[
                k, m, rows(me1 * r1, r1)
            ]
    o2_copy.wait_recv()
    o3_copy.wait_recv()
    for m in range(2):
        o2[:, m * half : (m + 1) * half] = o2s[m]
        o3[:, m * half : (m + 1) * half] = o3s[m]

    bend(1)
    collect(0)
    collect(1)

    for copy in copies:
        copy.wait_send()
    for k in range(2):

        @pl.loop(0, tile_chunks)
        def _(r):
            tile_copy(k, X, r, 0).wait_send()

            @pl.when(has_ahead)
            def _():
                tile_copy(k, Z_ON, r, 0).wait_send()
                tile_copy(k, DIAGONAL, r, 0).wait_send()

            @pl.when(has_behind)
            def _():
                tile_copy(k, Z_BACK, r, 0).wait_send()


def hand_over(*refs):
    count = (len(refs) - 2) // 3
    sources, goals, held = refs[:count], refs[count : 2 * count], refs[2 * count : 3 * count]
    in_sem, out_sem = refs[-2:]
    arriving = [
        pltpu.make_async_copy(sources[i], held[i], in_sem.at[i]) for i in range(count)
    ]
    leaving = [
        pltpu.make_async_copy(held[i], goals[i], out_sem.at[i]) for i in range(count)
    ]
    for copy in arriving:
        copy.start()
    for i in range(count):
        arriving[i].wait()
        leaving[i].start()
    for copy in leaving:
        copy.wait()


def local(
    leaf_load, leaf_inverse, leaf_coupling, leaf_rowmap,
    load_first, load_second, load_third,
    inverse_first, inverse_second, inverse_third,
    coupling_first, coupling_second, rowmap_first, rowmap_second,
    surface_coupling, neighbor_tiles,
):
    n = lax.axis_size("front")
    width = lax.axis_size("col")
    fr, panel = leaf_load.shape
    sep = leaf_coupling.shape[0]
    block = leaf_inverse.shape[0]
    tile = surface_coupling.shape[1]
    half, quarter = panel // 2, panel // 4
    r1, r2, r3 = inverse_first.shape[0], inverse_second.shape[0], inverse_third.shape[0]
    vmem = pl.BlockSpec(memory_space=pltpu.VMEM)
    hbm = pl.BlockSpec(memory_space=pl.ANY)

    def v(*shape, dtype=BF):
        return pltpu.VMEM(shape, dtype)

    results = pl.pallas_call(
        functools.partial(kernel, n),
        out_shape=[
            jax.ShapeDtypeStruct(s, BF)
            for s in ((fr, panel), (tile, panel), (r1, panel), (r2, panel), (r3, panel))
        ],
        in_specs=[hbm, vmem, hbm] + [vmem] * 12 + [hbm],
        out_specs=[vmem] * 5,
        scratch_shapes=[
            v(block * width, fr), v(fr, sep), v(fr, panel), v(sep, panel, dtype=F32),
            v(2, 2 * r1, sep), v(4, 2 * r2, sep), v(8, r3, sep),
            v(sep, half), v(sep, half), v(sep, half),
            v(fr, panel), v(sep, fr),
            v(2, sep, quarter), v(2, sep, quarter), v(2, sep, quarter), v(2, sep, quarter),
            v(2, sep, quarter), v(2, sep, quarter), v(2, sep, quarter), v(2, sep, quarter),
            v(sep, half), v(sep, half), v(2, 2, sep, quarter),
            v(2, r3, half), v(2, r2, half), v(fr, half), v(2, fr, half),
            v(*surface_coupling.shape), v(2, 4, tile, half), v(2, 3, tile, half), v(2, tile, half),
            pltpu.SemaphoreType.DMA((64,)), pltpu.SemaphoreType.DMA((64,)),
            pltpu.SemaphoreType.DMA((2, 4, tile // block)),
            pltpu.SemaphoreType.DMA((2, 4, tile // block)),
            pltpu.SemaphoreType.DMA((3,)),
        ],
        compiler_params=pltpu.CompilerParams(
            collective_id=0, has_side_effects=True, vmem_limit_bytes=56 * 1024 * 1024
        ),
        cost_estimate=pl.CostEstimate(
            flops=12 * fr * fr * panel, bytes_accessed=16 * fr * fr, transcendentals=0
        ),
    )(
        leaf_load, leaf_inverse, leaf_coupling, leaf_rowmap,
        load_first, load_second, load_third,
        inverse_first, inverse_second, inverse_third,
        coupling_first, coupling_second, rowmap_first, rowmap_second, neighbor_tiles.T,
        surface_coupling,
    )
    return pl.pallas_call(
        hand_over,
        out_shape=[jax.ShapeDtypeStruct(x.shape, x.dtype) for x in results],
        in_specs=[hbm] * 5,
        out_specs=[hbm] * 5,
        scratch_shapes=[v(*x.shape) for x in results]
        + [pltpu.SemaphoreType.DMA((5,)), pltpu.SemaphoreType.DMA((5,))],
        compiler_params=pltpu.CompilerParams(vmem_limit_bytes=60 * 1024 * 1024),
    )(*results)


def solution(mesh):
    return jax.shard_map(
        local,
        mesh=mesh,
        in_specs=(
            P("front", "col"), P(("front", "col"), None), P("front", None), P("front", None),
            P("front", "col"), P("front", "col"), P("front", "col"),
            P("front", None), P("front", None), P("front", None),
            P(None, "front"), P(None, "front"), P(), P(),
            P("front", None, None), P(),
        ),
        out_specs=(P("front", "col"),) * 5,
        check_vma=False,
    )
```

```python
import functools

import jax
import jax.numpy as jnp
from jax import lax
from jax.experimental import pallas as pl
from jax.experimental.pallas import tpu as pltpu
from jax.sharding import PartitionSpec as P

BF = jnp.bfloat16
F32 = jnp.float32
MESH = pl.DeviceIdType.MESH
X, Z_ON, Z_BACK, DIAGONAL = range(4)


def mm(a, b):
    return jnp.dot(a, b, preferred_element_type=F32)


def tmm(a, b):
    return lax.dot_general(a, b, (((0,), (0,)), ((), ())), preferred_element_type=F32)


def flip(x, bit):
    return x + bit * (1 - 2 * ((x // bit) % 2))


def kernel(
    n, b_hbm, g_ref, c_hbm, map0, l1, l2, l3, i1, i2, i3, d_ref, e_ref, map1, map2, tile_ref, a_hbm,
    vol, tiles, o1, o2, o3,
    gf, ct, start, part, w1, w2, w3, l1f, l2f, l3f,
    b_ref, c_ref, give1, x1, y1, p2, x2, y2, p3, x3, s3, s2, s1, o3s, o2s, pull, value, av, stage, got, bent,
    send_sem, recv_sem, tile_send, tile_recv, load_sem,
):
    f = lax.axis_index("front")
    c = lax.axis_index("col")
    core = c % 2
    ca, cb = flip(c, 1), flip(c, 2)
    cd = flip(ca, 2)
    b0, b1 = f % 2, (f // 2) % 2
    fx, fy, fz = flip(f, 1), flip(f, 2), flip(f, 4)
    sep = l1f.shape[0]
    panel = b_ref.shape[1]
    half, quarter = panel // 2, panel // 4
    block = g_ref.shape[0]
    r1, r2, r3 = i1.shape[0], i2.shape[0], i3.shape[0]

    def cols(at, size):
        return pl.ds(pl.multiple_of(at, 128), size)

    def rows(at, size):
        return pl.ds(pl.multiple_of(at, 16), size)

    def half_of(g):
        return cols((g % 2) * half, half)

    copies = []

    def send(src, dst, **where):
        i = len(copies)
        copy = pltpu.make_async_remote_copy(
            src_ref=src, dst_ref=dst, send_sem=send_sem.at[i], recv_sem=recv_sem.at[i],
            device_id=where, device_id_type=MESH,
        )
        copies.append(copy)
        copy.start()
        return copy

    loads = [
        pltpu.make_async_copy(src, dst, load_sem.at[i])
        for i, (src, dst) in enumerate(((b_hbm, b_ref), (c_hbm, c_ref), (a_hbm, av)))
    ]
    loads[0].start()
    loads[1].start()

    barrier = pltpu.get_barrier_semaphore()
    for other in (ca, cb):
        pl.semaphore_signal(barrier, inc=1, device_id={"col": other}, device_id_type=MESH)
    for other in (fx, fy, fz):
        pl.semaphore_signal(barrier, inc=1, device_id={"front": other}, device_id_type=MESH)
    ahead = f + 2 * (2 * b0 - 1)
    behind = f - 2 * (2 * b0 - 1)
    has_ahead = jnp.logical_and(ahead >= 0, ahead < n)
    has_behind = jnp.logical_and(behind >= 0, behind < n)
    for ok, other in ((has_ahead, ahead), (has_behind, behind)):

        @pl.when(ok)
        def _(other=other):
            pl.semaphore_signal(barrier, inc=1, device_id={"front": other}, device_id_type=MESH)
    count = 5 + has_ahead.astype(jnp.int32) + has_behind.astype(jnp.int32)
    pl.semaphore_wait(barrier, count)

    own_rows = rows(c * block, block)
    piece = block // 2
    g_far = [
        send(g_ref.at[pl.ds(k * piece, piece)], gf.at[rows(c * block + k * piece, piece)], col=cb)
        for k in range(2)
    ]
    g_near = send(g_ref, gf.at[own_rows], col=ca)
    loads[2].start()

    lines = lax.broadcasted_iota(jnp.int32, (sep, sep), 0)

    def chooser(row):
        return (lines == row).astype(F32).astype(BF)

    me1, me2, me3 = f % 2, f % 4, f % 8
    pair2, pair3, four3 = me2 - b0, me3 - b0, (me3 // 4) * 4
    in1, in2, in3 = rows(core * r1, r1), rows(core * r2, r2), rows(core * (r3 // 2), r3 // 2)
    w2[me2, 0:r2] = i2[...]
    w2[me2, r2 : 2 * r2] = tmm(e_ref[...], chooser(map2[pl.ds(f // 4, 1), :])).astype(BF)
    w3[me3] = i3[...]
    w2_x = send(w2.at[me2, in2], w2.at[me2, in2], front=fx)
    l2_x = send(l2.at[:, half_of(fx)], l2f.at[rows(me2 * r2, r2)], front=fx)
    w3_x = send(w3.at[me3, in3], w3.at[me3, in3], front=fx)
    l3_x = send(l3.at[:, half_of(fx)], l3f.at[rows(me3 * r3, r3)], front=fx)
    w1[me1, 0:r1] = i1[...]
    w1[me1, r1 : 2 * r1] = tmm(d_ref[...], chooser(map1[pl.ds(f // 2, 1), :])).astype(BF)
    w1_copy = send(w1.at[me1, in1], w1.at[me1, in1], front=fx)
    l1_copy = send(l1.at[:, half_of(fx)], l1f.at[rows(b0 * r1, r1)], front=fx)
    gf[own_rows] = g_ref[...]
    l1f[rows(b0 * r1, r1)] = l1[:, half_of(f)]
    l2f[rows(me2 * r2, r2)] = l2[:, half_of(f)]
    l3f[rows(me3 * r3, r3)] = l3[:, half_of(f)]

    @pl.when(jnp.logical_not(has_behind))
    def _():
        got[:, Z_ON] = jnp.zeros((2,) + got.shape[2:], BF)
        bent[...] = jnp.zeros(bent.shape, BF)

    @pl.when(jnp.logical_not(has_ahead))
    def _():
        got[:, Z_BACK] = jnp.zeros((2,) + got.shape[2:], BF)

    loads[1].wait()
    ct[...] = tmm(c_ref[...], chooser(map0[...])).astype(BF)

    def leaf(slot, first=False):
        at = rows(slot * block, block)
        solved = mm(gf[at], b_ref[...]).astype(BF)
        start[at] = solved
        term = tmm(ct[at], solved)
        part[...] = term if first else part[...] + term

    loads[0].wait()
    leaf(c, True)
    g_near.wait_recv()
    leaf(ca)
    for copy in (w2_x, l2_x, w3_x, l3_x):
        copy.wait_recv()
    two = w2.at[pl.ds(pair2, 2), in2]
    w2_y = send(two, two, front=fy)
    two = l2f.at[rows(pair2 * r2, 2 * r2)]
    l2_y = send(two, two, front=fy)
    two = w3.at[pl.ds(pair3, 2), in3]
    w3_y = send(two, two, front=fy)
    two = l3f.at[rows(pair3 * r3, 2 * r3)]
    l3_y = send(two, two, front=fy)
    g_pass = []
    for k in range(2):
        g_far[k].wait_recv()
        at = rows(cb * block + k * piece, piece)
        g_pass.append(send(gf.at[at], gf.at[at], col=ca))
    one = w2.at[flip(me2, 1), in2]
    w2_pass = [send(one, one, col=ca)]
    one = w3.at[flip(me3, 1), in3]
    w3_pass = [send(one, one, col=ca)]
    leaf(cb)
    w1_copy.wait_recv()
    one = w1.at[1 - me1, in1]
    w1_pass = send(one, one, col=ca)
    for k in range(2):
        g_pass[k].wait_recv()
    leaf(cd)

    def joined(w, at, size):
        return jnp.concatenate([w[m, at : at + size] for m in range(w.shape[0])], axis=0)

    def in_half(k):
        return pl.ds(k * quarter, quarter)

    def in_panel(which, k):
        return cols(which * half + k * quarter, quarter)

    x1_copies = []
    for k in range(2):
        give1[k] = part[:, in_panel(1 - b0, k)].astype(BF)
        x1_copies.append(send(give1.at[k], x1.at[k], front=fx))
    for copy in (w2_y, w3_y, l3_y):
        copy.wait_recv()
    four = w3.at[pl.ds(four3, 4), in3]
    w3_z = send(four, four, front=fz)
    four = l3f.at[rows(four3 * r3, 4 * r3)]
    l3_z = send(four, four, front=fz)
    two = w2.at[pl.ds(2 - pair2, 2), in2]
    w2_pass.append(send(two, two, col=ca))
    two = w3.at[pl.ds(four3 + 2 - (pair3 - four3), 2), in3]
    w3_pass.append(send(two, two, col=ca))
    l1_copy.wait_recv()
    w1_pass.wait_recv()
    x2_copies = []
    for k in range(2):
        x1_copies[k].wait_recv()
        rhs = l1f[:, in_half(k)].astype(F32) - part[:, in_panel(b0, k)] - x1[k].astype(F32)
        y1[k] = mm(joined(w1, 0, r1), rhs.astype(BF)).astype(BF)
        p2[k] = tmm(joined(w1, r1, r1), y1[k]).astype(BF)
        x2_copies.append(send(p2.at[k], x2.at[k], front=fy))
    for copy in [l2_y] + w2_pass:
        copy.wait_recv()
    x3_copies = []
    for k in range(2):
        x2_copies[k].wait_recv()
        rhs = l2f[:, in_half(k)].astype(F32) - p2[k].astype(F32) - x2[k].astype(F32)
        y2[k] = mm(joined(w2, 0, r2), rhs.astype(BF)).astype(BF)
        p3[k] = tmm(joined(w2, r2, r2), y2[k]).astype(BF)
        x3_copies.append(send(p3.at[k], x3.at[k], front=fz))
    w3_z.wait_recv()
    four = w3.at[pl.ds(4 - four3, 4), in3]
    w3_pass.append(send(four, four, col=ca))
    for copy in [l3_z] + w3_pass:
        copy.wait_recv()

    s1_copies = []
    for k in range(2):
        x3_copies[k].wait_recv()
        rhs = l3f[:, in_half(k)].astype(F32) - p3[k].astype(F32) - x3[k].astype(F32)
        top = mm(joined(w3, 0, r3), rhs.astype(BF)).astype(BF)
        s3[:, in_half(k)] = top
        pull2 = mm(joined(w2, r2, r2), top).astype(BF)
        second = (y2[k].astype(F32) - mm(joined(w2, 0, r2), pull2)).astype(BF)
        s2[:, in_half(k)] = second
        pull1 = mm(joined(w1, r1, r1), second).astype(BF)
        s1[k, b0] = (y1[k].astype(F32) - mm(joined(w1, 0, r1), pull1)).astype(BF)
        s1_copies.append(send(s1.at[k, b0], s1.at[k, b0], front=fx))
    o3_copy = send(s3.at[rows((fx % 8) * r3, r3)], o3s.at[b0], front=fx)
    o2_copy = send(s2.at[rows((fx % 4) * r2, r2)], o2s.at[b0], front=fx)
    loads[2].wait()

    chunk = block
    chunks = gf.shape[0] // chunk
    tile_chunks = got.shape[2] // chunk
    aimed = jnp.sum(
        jnp.where(
            lax.broadcasted_iota(jnp.int32, tile_ref.shape, 1) == f,
            tile_ref[...].astype(F32), 0.0,
        ),
        axis=1, keepdims=True,
    )
    aimed_a = jnp.broadcast_to(aimed[0:1], (chunk, half))
    aimed_b = jnp.broadcast_to(aimed[1:2], (chunk, half))
    goals = (fx, ahead, behind, fx + ahead - f)

    sub = chunk // 2

    def tile_copy(k, kind, r, parity, h):
        at = rows(r * chunk + h * sub, sub)
        if kind == DIAGONAL:
            target, landing = (fx if parity else ahead), bent.at[k, at]
        else:
            target, landing = goals[kind], got.at[k, kind, at]
        return pltpu.make_async_remote_copy(
            src_ref=stage.at[k, kind, at], dst_ref=landing,
            send_sem=tile_send.at[k, kind, 2 * r + h], recv_sem=tile_recv.at[k, kind, 2 * r + h],
            device_id={"front": target}, device_id_type=MESH,
        )

    def volume(k):
        s1_copies[k].wait_recv()
        both = jnp.concatenate([s1[k, 0], s1[k, 1]], axis=1)

        @pl.loop(0, chunks)
        def _(r):
            at = rows(r * chunk, chunk)
            pull[at] = mm(ct[at], both).astype(BF)

        @pl.loop(0, chunks)
        def _(r):
            at = rows(r * chunk, chunk)
            change = mm(gf[at], pull[...])
            for m in range(2):
                here = pl.ds(m * half + k * quarter, quarter)
                new = (
                    start[at, here].astype(F32) - change[:, m * quarter : (m + 1) * quarter]
                ).astype(BF)
                vol[at, here] = new
                value[k, at, pl.ds(m * quarter, quarter)] = new

    def contribute(k):
        @pl.loop(0, tile_chunks // 2)
        def _(pair):
            for parity in range(2):
                r = pair * 2 + parity
                at = rows(r * chunk, chunk)
                first = mm(av[1, at], value[k])
                second = mm(av[2, at], value[k])
                for kind in (DIAGONAL, X, Z_ON, Z_BACK):
                    goal = goals[kind].astype(F32)
                    stage[k, kind, at] = jnp.where(
                        aimed_a == goal, first, jnp.where(aimed_b == goal, second, 0.0)
                    ).astype(BF)

                @pl.when(has_ahead)
                def _():
                    for kind in (DIAGONAL, Z_ON):
                        for h in range(2):
                            tile_copy(k, kind, r, parity, h).start()

                if parity:
                    for h in range(2):
                        tile_copy(k, X, r, parity, h).start()
                else:

                    @pl.when(has_behind)
                    def _():
                        for h in range(2):
                            tile_copy(k, Z_BACK, r, parity, h).start()

    def bend(k):
        @pl.loop(0, tile_chunks // 2)
        def _(pair):
            for parity in range(2):
                r = pair * 2 + parity
                kind = Z_BACK if parity else X
                for h in range(2):
                    at = rows(r * chunk + h * sub, sub)

                    @pl.when(has_behind)
                    def _():
                        tile_copy(k, DIAGONAL, r, parity, h).wait_recv()

                    stage[k, kind, at] = (
                        stage[k, kind, at].astype(F32) + bent[k, at].astype(F32)
                    ).astype(BF)
                    if parity:

                        @pl.when(has_behind)
                        def _():
                            tile_copy(k, Z_BACK, r, parity, h).start()
                    else:
                        tile_copy(k, X, r, parity, h).start()

    def collect(k):
        @pl.loop(0, tile_chunks)
        def _(r):
            at = rows(r * chunk, chunk)
            total = mm(av[0, at], value[k])
            for h in range(2):
                tile_copy(k, X, r, 0, h).wait_recv()

            @pl.when(has_behind)
            def _():
                for h in range(2):
                    tile_copy(k, Z_ON, r, 0, h).wait_recv()

            @pl.when(has_ahead)
            def _():
                for h in range(2):
                    tile_copy(k, Z_BACK, r, 0, h).wait_recv()

            for kind in (X, Z_ON, Z_BACK):
                total = total + got[k, kind, at].astype(F32)
            for m in range(2):
                tiles[at, pl.ds(m * half + k * quarter, quarter)] = total[
                    :, m * quarter : (m + 1) * quarter
                ].astype(BF)

    volume(0)
    contribute(0)
    volume(1)
    bend(0)
    contribute(1)

    o3s[b0] = s3[rows(me3 * r3, r3)]
    o2s[b0] = s2[rows(me2 * r2, r2)]
    for k in range(2):
        for m in range(2):
            o1[:, m * half + k * quarter : m * half + (k + 1) * quarter] = s1[
                k, m, rows(me1 * r1, r1)
            ]
    o2_copy.wait_recv()
    o3_copy.wait_recv()
    for m in range(2):
        o2[:, m * half : (m + 1) * half] = o2s[m]
        o3[:, m * half : (m + 1) * half] = o3s[m]

    bend(1)
    collect(0)
    collect(1)

    for copy in copies:
        copy.wait_send()
    for k in range(2):

        @pl.loop(0, tile_chunks)
        def _(r):
            for h in range(2):
                tile_copy(k, X, r, 0, h).wait_send()

            @pl.when(has_ahead)
            def _():
                for h in range(2):
                    tile_copy(k, Z_ON, r, 0, h).wait_send()
                    tile_copy(k, DIAGONAL, r, 0, h).wait_send()

            @pl.when(has_behind)
            def _():
                for h in range(2):
                    tile_copy(k, Z_BACK, r, 0, h).wait_send()


def hand_over(*refs):
    count = (len(refs) - 2) // 3
    sources, goals, held = refs[:count], refs[count : 2 * count], refs[2 * count : 3 * count]
    in_sem, out_sem = refs[-2:]
    arriving = [
        pltpu.make_async_copy(sources[i], held[i], in_sem.at[i]) for i in range(count)
    ]
    leaving = [
        pltpu.make_async_copy(held[i], goals[i], out_sem.at[i]) for i in range(count)
    ]
    for copy in arriving:
        copy.start()
    for i in range(count):
        arriving[i].wait()
        leaving[i].start()
    for copy in leaving:
        copy.wait()


def local(
    leaf_load, leaf_inverse, leaf_coupling, leaf_rowmap,
    load_first, load_second, load_third,
    inverse_first, inverse_second, inverse_third,
    coupling_first, coupling_second, rowmap_first, rowmap_second,
    surface_coupling, neighbor_tiles,
):
    n = lax.axis_size("front")
    width = lax.axis_size("col")
    fr, panel = leaf_load.shape
    sep = leaf_coupling.shape[0]
    block = leaf_inverse.shape[0]
    tile = surface_coupling.shape[1]
    half, quarter = panel // 2, panel // 4
    r1, r2, r3 = inverse_first.shape[0], inverse_second.shape[0], inverse_third.shape[0]
    vmem = pl.BlockSpec(memory_space=pltpu.VMEM)
    hbm = pl.BlockSpec(memory_space=pl.ANY)

    def v(*shape, dtype=BF):
        return pltpu.VMEM(shape, dtype)

    results = pl.pallas_call(
        functools.partial(kernel, n),
        out_shape=[
            jax.ShapeDtypeStruct(s, BF)
            for s in ((fr, panel), (tile, panel), (r1, panel), (r2, panel), (r3, panel))
        ],
        in_specs=[hbm, vmem, hbm] + [vmem] * 12 + [hbm],
        out_specs=[vmem] * 5,
        scratch_shapes=[
            v(block * width, fr), v(fr, sep), v(fr, panel), v(sep, panel, dtype=F32),
            v(2, 2 * r1, sep), v(4, 2 * r2, sep), v(8, r3, sep),
            v(sep, half), v(sep, half), v(sep, half),
            v(fr, panel), v(sep, fr),
            v(2, sep, quarter), v(2, sep, quarter), v(2, sep, quarter), v(2, sep, quarter),
            v(2, sep, quarter), v(2, sep, quarter), v(2, sep, quarter), v(2, sep, quarter),
            v(sep, half), v(sep, half), v(2, 2, sep, quarter),
            v(2, r3, half), v(2, r2, half), v(fr, half), v(2, fr, half),
            v(*surface_coupling.shape), v(2, 4, tile, half), v(2, 3, tile, half), v(2, tile, half),
            pltpu.SemaphoreType.DMA((64,)), pltpu.SemaphoreType.DMA((64,)),
            pltpu.SemaphoreType.DMA((2, 4, 2 * tile // block)),
            pltpu.SemaphoreType.DMA((2, 4, 2 * tile // block)),
            pltpu.SemaphoreType.DMA((3,)),
        ],
        compiler_params=pltpu.CompilerParams(
            collective_id=0, has_side_effects=True, vmem_limit_bytes=56 * 1024 * 1024
        ),
        cost_estimate=pl.CostEstimate(
            flops=12 * fr * fr * panel, bytes_accessed=16 * fr * fr, transcendentals=0
        ),
    )(
        leaf_load, leaf_inverse, leaf_coupling, leaf_rowmap,
        load_first, load_second, load_third,
        inverse_first, inverse_second, inverse_third,
        coupling_first, coupling_second, rowmap_first, rowmap_second, neighbor_tiles.T,
        surface_coupling,
    )
    return pl.pallas_call(
        hand_over,
        out_shape=[jax.ShapeDtypeStruct(x.shape, x.dtype) for x in results],
        in_specs=[hbm] * 5,
        out_specs=[hbm] * 5,
        scratch_shapes=[v(*x.shape) for x in results]
        + [pltpu.SemaphoreType.DMA((5,)), pltpu.SemaphoreType.DMA((5,))],
        compiler_params=pltpu.CompilerParams(vmem_limit_bytes=60 * 1024 * 1024),
    )(*results)


def solution(mesh):
    return jax.shard_map(
        local,
        mesh=mesh,
        in_specs=(
            P("front", "col"), P(("front", "col"), None), P("front", None), P("front", None),
            P("front", "col"), P("front", "col"), P("front", "col"),
            P("front", None), P("front", None), P("front", None),
            P(None, "front"), P(None, "front"), P(), P(),
            P("front", None, None), P(),
        ),
        out_specs=(P("front", "col"),) * 5,
        check_vma=False,
    )
```

```python
import functools

import jax
import jax.numpy as jnp
from jax import lax
from jax.experimental import pallas as pl
from jax.experimental.pallas import tpu as pltpu
from jax.sharding import PartitionSpec as P

BF = jnp.bfloat16
F32 = jnp.float32
MESH = pl.DeviceIdType.MESH
X, Z_ON, Z_BACK, DIAGONAL = range(4)


def mm(a, b):
    return jnp.dot(a, b, preferred_element_type=F32)


def tmm(a, b):
    return lax.dot_general(a, b, (((0,), (0,)), ((), ())), preferred_element_type=F32)


def flip(x, bit):
    return x + bit * (1 - 2 * ((x // bit) % 2))


def kernel(
    n, b_hbm, g_ref, c_hbm, map0, l1, l2, l3, i1, i2, i3, d_ref, e_ref, map1, map2, tile_ref, a_hbm,
    vol, tiles, o1, o2, o3,
    gf, ct, start, part, w1, w2, w3, l1f, l2f, l3f,
    b_ref, c_ref, give1, x1, y1, p2, x2, y2, p3, x3, s3, s2, s1, o3s, o2s, pull, value, av, stage, got, bent,
    send_sem, recv_sem, tile_send, tile_recv, load_sem,
):
    f = lax.axis_index("front")
    c = lax.axis_index("col")
    core = c % 2
    ca, cb = flip(c, 1), flip(c, 2)
    cd = flip(ca, 2)
    b0, b1 = f % 2, (f // 2) % 2
    fx, fy, fz = flip(f, 1), flip(f, 2), flip(f, 4)
    sep = l1f.shape[0]
    panel = b_ref.shape[1]
    half, quarter = panel // 2, panel // 4
    block = g_ref.shape[0]
    r1, r2, r3 = i1.shape[0], i2.shape[0], i3.shape[0]

    def cols(at, size):
        return pl.ds(pl.multiple_of(at, 128), size)

    def rows(at, size):
        return pl.ds(pl.multiple_of(at, 16), size)

    def half_of(g):
        return cols((g % 2) * half, half)

    copies = []

    def send(src, dst, **where):
        i = len(copies)
        copy = pltpu.make_async_remote_copy(
            src_ref=src, dst_ref=dst, send_sem=send_sem.at[i], recv_sem=recv_sem.at[i],
            device_id=where, device_id_type=MESH,
        )
        copies.append(copy)
        copy.start()
        return copy

    loads = [
        pltpu.make_async_copy(src, dst, load_sem.at[i])
        for i, (src, dst) in enumerate(((b_hbm, b_ref), (c_hbm, c_ref), (a_hbm, av)))
    ]
    for load in loads:
        load.start()

    barrier = pltpu.get_barrier_semaphore()
    for other in (ca, cb):
        pl.semaphore_signal(barrier, inc=1, device_id={"col": other}, device_id_type=MESH)
    for other in (fx, fy, fz):
        pl.semaphore_signal(barrier, inc=1, device_id={"front": other}, device_id_type=MESH)
    ahead = f + 2 * (2 * b0 - 1)
    behind = f - 2 * (2 * b0 - 1)
    has_ahead = jnp.logical_and(ahead >= 0, ahead < n)
    has_behind = jnp.logical_and(behind >= 0, behind < n)
    for ok, other in ((has_ahead, ahead), (has_behind, behind)):

        @pl.when(ok)
        def _(other=other):
            pl.semaphore_signal(barrier, inc=1, device_id={"front": other}, device_id_type=MESH)
    count = 5 + has_ahead.astype(jnp.int32) + has_behind.astype(jnp.int32)
    pl.semaphore_wait(barrier, count)

    own_rows = rows(c * block, block)
    g_near = send(g_ref, gf.at[own_rows], col=ca)
    piece = block // 2
    g_far = [
        send(g_ref.at[pl.ds(k * piece, piece)], gf.at[rows(c * block + k * piece, piece)], col=cb)
        for k in range(2)
    ]

    lines = lax.broadcasted_iota(jnp.int32, (sep, sep), 0)

    def chooser(row):
        return (lines == row).astype(F32).astype(BF)

    me1, me2, me3 = f % 2, f % 4, f % 8
    pair2, pair3, four3 = me2 - b0, me3 - b0, (me3 // 4) * 4
    in1, in2, in3 = rows(core * r1, r1), rows(core * r2, r2), rows(core * (r3 // 2), r3 // 2)
    w2[me2, 0:r2] = i2[...]
    w2[me2, r2 : 2 * r2] = tmm(e_ref[...], chooser(map2[pl.ds(f // 4, 1), :])).astype(BF)
    w3[me3] = i3[...]
    w2_x = send(w2.at[me2, in2], w2.at[me2, in2], front=fx)
    l2_x = send(l2.at[:, half_of(fx)], l2f.at[rows(me2 * r2, r2)], front=fx)
    w3_x = send(w3.at[me3, in3], w3.at[me3, in3], front=fx)
    l3_x = send(l3.at[:, half_of(fx)], l3f.at[rows(me3 * r3, r3)], front=fx)
    w1[me1, 0:r1] = i1[...]
    w1[me1, r1 : 2 * r1] = tmm(d_ref[...], chooser(map1[pl.ds(f // 2, 1), :])).astype(BF)
    w1_copy = send(w1.at[me1, in1], w1.at[me1, in1], front=fx)
    l1_copy = send(l1.at[:, half_of(fx)], l1f.at[rows(b0 * r1, r1)], front=fx)
    gf[own_rows] = g_ref[...]
    l1f[rows(b0 * r1, r1)] = l1[:, half_of(f)]
    l2f[rows(me2 * r2, r2)] = l2[:, half_of(f)]
    l3f[rows(me3 * r3, r3)] = l3[:, half_of(f)]

    @pl.when(jnp.logical_not(has_behind))
    def _():
        got[:, Z_ON] = jnp.zeros((2,) + got.shape[2:], BF)
        bent[...] = jnp.zeros(bent.shape, BF)

    @pl.when(jnp.logical_not(has_ahead))
    def _():
        got[:, Z_BACK] = jnp.zeros((2,) + got.shape[2:], BF)

    loads[1].wait()
    ct[...] = tmm(c_ref[...], chooser(map0[...])).astype(BF)

    def leaf(slot, first=False):
        at = rows(slot * block, block)
        solved = mm(gf[at], b_ref[...]).astype(BF)
        start[at] = solved
        term = tmm(ct[at], solved)
        part[...] = term if first else part[...] + term

    loads[0].wait()
    leaf(c, True)
    g_near.wait_recv()
    leaf(ca)
    for copy in (w2_x, l2_x, w3_x, l3_x):
        copy.wait_recv()
    two = w2.at[pl.ds(pair2, 2), in2]
    w2_y = send(two, two, front=fy)
    two = l2f.at[rows(pair2 * r2, 2 * r2)]
    l2_y = send(two, two, front=fy)
    two = w3.at[pl.ds(pair3, 2), in3]
    w3_y = send(two, two, front=fy)
    two = l3f.at[rows(pair3 * r3, 2 * r3)]
    l3_y = send(two, two, front=fy)
    g_pass = []
    for k in range(2):
        g_far[k].wait_recv()
        at = rows(cb * block + k * piece, piece)
        g_pass.append(send(gf.at[at], gf.at[at], col=ca))
    one = w2.at[flip(me2, 1), in2]
    w2_pass = [send(one, one, col=ca)]
    one = w3.at[flip(me3, 1), in3]
    w3_pass = [send(one, one, col=ca)]
    leaf(cb)
    w1_copy.wait_recv()
    one = w1.at[1 - me1, in1]
    w1_pass = send(one, one, col=ca)
    for k in range(2):
        g_pass[k].wait_recv()
    leaf(cd)

    def joined(w, at, size):
        return jnp.concatenate([w[m, at : at + size] for m in range(w.shape[0])], axis=0)

    def in_half(k):
        return pl.ds(k * quarter, quarter)

    def in_panel(which, k):
        return cols(which * half + k * quarter, quarter)

    x1_copies = []
    for k in range(2):
        give1[k] = part[:, in_panel(1 - b0, k)].astype(BF)
        x1_copies.append(send(give1.at[k], x1.at[k], front=fx))
    for copy in (w2_y, w3_y, l3_y):
        copy.wait_recv()
    four = w3.at[pl.ds(four3, 4), in3]
    w3_z = send(four, four, front=fz)
    four = l3f.at[rows(four3 * r3, 4 * r3)]
    l3_z = send(four, four, front=fz)
    two = w2.at[pl.ds(2 - pair2, 2), in2]
    w2_pass.append(send(two, two, col=ca))
    two = w3.at[pl.ds(four3 + 2 - (pair3 - four3), 2), in3]
    w3_pass.append(send(two, two, col=ca))
    l1_copy.wait_recv()
    w1_pass.wait_recv()
    x2_copies = []
    for k in range(2):
        x1_copies[k].wait_recv()
        rhs = l1f[:, in_half(k)].astype(F32) - part[:, in_panel(b0, k)] - x1[k].astype(F32)
        y1[k] = mm(joined(w1, 0, r1), rhs.astype(BF)).astype(BF)
        p2[k] = tmm(joined(w1, r1, r1), y1[k]).astype(BF)
        x2_copies.append(send(p2.at[k], x2.at[k], front=fy))
    for copy in [l2_y] + w2_pass:
        copy.wait_recv()
    x3_copies = []
    for k in range(2):
        x2_copies[k].wait_recv()
        rhs = l2f[:, in_half(k)].astype(F32) - p2[k].astype(F32) - x2[k].astype(F32)
        y2[k] = mm(joined(w2, 0, r2), rhs.astype(BF)).astype(BF)
        p3[k] = tmm(joined(w2, r2, r2), y2[k]).astype(BF)
        x3_copies.append(send(p3.at[k], x3.at[k], front=fz))
    w3_z.wait_recv()
    four = w3.at[pl.ds(4 - four3, 4), in3]
    w3_pass.append(send(four, four, col=ca))
    for copy in [l3_z] + w3_pass:
        copy.wait_recv()

    s1_copies = []
    for k in range(2):
        x3_copies[k].wait_recv()
        rhs = l3f[:, in_half(k)].astype(F32) - p3[k].astype(F32) - x3[k].astype(F32)
        top = mm(joined(w3, 0, r3), rhs.astype(BF)).astype(BF)
        s3[:, in_half(k)] = top
        pull2 = mm(joined(w2, r2, r2), top).astype(BF)
        second = (y2[k].astype(F32) - mm(joined(w2, 0, r2), pull2)).astype(BF)
        s2[:, in_half(k)] = second
        pull1 = mm(joined(w1, r1, r1), second).astype(BF)
        s1[k, b0] = (y1[k].astype(F32) - mm(joined(w1, 0, r1), pull1)).astype(BF)
        s1_copies.append(send(s1.at[k, b0], s1.at[k, b0], front=fx))
    o3_copy = send(s3.at[rows((fx % 8) * r3, r3)], o3s.at[b0], front=fx)
    o2_copy = send(s2.at[rows((fx % 4) * r2, r2)], o2s.at[b0], front=fx)
    loads[2].wait()

    chunk = block
    chunks = gf.shape[0] // chunk
    tile_chunks = got.shape[2] // chunk
    aimed = jnp.sum(
        jnp.where(
            lax.broadcasted_iota(jnp.int32, tile_ref.shape, 1) == f,
            tile_ref[...].astype(F32), 0.0,
        ),
        axis=1, keepdims=True,
    )
    aimed_a = jnp.broadcast_to(aimed[0:1], (chunk, half))
    aimed_b = jnp.broadcast_to(aimed[1:2], (chunk, half))
    goals = (fx, ahead, behind, fx + ahead - f)

    def tile_copy(k, kind, r, parity):
        at = rows(r * chunk, chunk)
        if kind == DIAGONAL:
            target, landing = (fx if parity else ahead), bent.at[k, at]
        else:
            target, landing = goals[kind], got.at[k, kind, at]
        return pltpu.make_async_remote_copy(
            src_ref=stage.at[k, kind, at], dst_ref=landing,
            send_sem=tile_send.at[k, kind, r], recv_sem=tile_recv.at[k, kind, r],
            device_id={"front": target}, device_id_type=MESH,
        )

    def volume(k):
        s1_copies[k].wait_recv()
        both = jnp.concatenate([s1[k, 0], s1[k, 1]], axis=1)

        @pl.loop(0, chunks)
        def _(r):
            at = rows(r * chunk, chunk)
            pull[at] = mm(ct[at], both).astype(BF)

        @pl.loop(0, chunks)
        def _(r):
            at = rows(r * chunk, chunk)
            change = mm(gf[at], pull[...])
            for m in range(2):
                here = pl.ds(m * half + k * quarter, quarter)
                new = (
                    start[at, here].astype(F32) - change[:, m * quarter : (m + 1) * quarter]
                ).astype(BF)
                vol[at, here] = new
                value[k, at, pl.ds(m * quarter, quarter)] = new

    def contribute(k):
        @pl.loop(0, tile_chunks // 2)
        def _(pair):
            for parity in range(2):
                r = pair * 2 + parity
                at = rows(r * chunk, chunk)
                first = mm(av[1, at], value[k])
                second = mm(av[2, at], value[k])
                for kind in (DIAGONAL, X, Z_ON, Z_BACK):
                    goal = goals[kind].astype(F32)
                    stage[k, kind, at] = jnp.where(
                        aimed_a == goal, first, jnp.where(aimed_b == goal, second, 0.0)
                    ).astype(BF)

                @pl.when(has_ahead)
                def _():
                    tile_copy(k, DIAGONAL, r, parity).start()
                    tile_copy(k, Z_ON, r, parity).start()

                if parity:
                    tile_copy(k, X, r, parity).start()
                else:

                    @pl.when(has_behind)
                    def _():
                        tile_copy(k, Z_BACK, r, parity).start()

    def bend(k):
        @pl.loop(0, tile_chunks // 2)
        def _(pair):
            for parity in range(2):
                r = pair * 2 + parity
                at = rows(r * chunk, chunk)
                kind = Z_BACK if parity else X

                @pl.when(has_behind)
                def _():
                    tile_copy(k, DIAGONAL, r, parity).wait_recv()

                stage[k, kind, at] = (
                    stage[k, kind, at].astype(F32) + bent[k, at].astype(F32)
                ).astype(BF)
                if parity:

                    @pl.when(has_behind)
                    def _():
                        tile_copy(k, Z_BACK, r, parity).start()
                else:
                    tile_copy(k, X, r, parity).start()

    def collect(k):
        @pl.loop(0, tile_chunks)
        def _(r):
            at = rows(r * chunk, chunk)
            total = mm(av[0, at], value[k])
            tile_copy(k, X, r, 0).wait_recv()

            @pl.when(has_behind)
            def _():
                tile_copy(k, Z_ON, r, 0).wait_recv()

            @pl.when(has_ahead)
            def _():
                tile_copy(k, Z_BACK, r, 0).wait_recv()

            for kind in (X, Z_ON, Z_BACK):
                total = total + got[k, kind, at].astype(F32)
            for m in range(2):
                tiles[at, pl.ds(m * half + k * quarter, quarter)] = total[
                    :, m * quarter : (m + 1) * quarter
                ].astype(BF)

    volume(0)
    contribute(0)
    volume(1)
    contribute(1)
    bend(0)

    o3s[b0] = s3[rows(me3 * r3, r3)]
    o2s[b0] = s2[rows(me2 * r2, r2)]
    for k in range(2):
        for m in range(2):
            o1[:, m * half + k * quarter : m * half + (k + 1) * quarter] = s1[
                k, m, rows(me1 * r1, r1)
            ]
    o2_copy.wait_recv()
    o3_copy.wait_recv()
    for m in range(2):
        o2[:, m * half : (m + 1) * half] = o2s[m]
        o3[:, m * half : (m + 1) * half] = o3s[m]

    bend(1)
    collect(0)
    collect(1)

    for copy in copies:
        copy.wait_send()
    for k in range(2):

        @pl.loop(0, tile_chunks)
        def _(r):
            tile_copy(k, X, r, 0).wait_send()

            @pl.when(has_ahead)
            def _():
                tile_copy(k, Z_ON, r, 0).wait_send()
                tile_copy(k, DIAGONAL, r, 0).wait_send()

            @pl.when(has_behind)
            def _():
                tile_copy(k, Z_BACK, r, 0).wait_send()


def hand_over(*refs):
    count = (len(refs) - 2) // 3
    sources, goals, held = refs[:count], refs[count : 2 * count], refs[2 * count : 3 * count]
    in_sem, out_sem = refs[-2:]
    arriving = [
        pltpu.make_async_copy(sources[i], held[i], in_sem.at[i]) for i in range(count)
    ]
    leaving = [
        pltpu.make_async_copy(held[i], goals[i], out_sem.at[i]) for i in range(count)
    ]
    for copy in arriving:
        copy.start()
    for i in range(count):
        arriving[i].wait()
        leaving[i].start()
    for copy in leaving:
        copy.wait()


def local(
    leaf_load, leaf_inverse, leaf_coupling, leaf_rowmap,
    load_first, load_second, load_third,
    inverse_first, inverse_second, inverse_third,
    coupling_first, coupling_second, rowmap_first, rowmap_second,
    surface_coupling, neighbor_tiles,
):
    n = lax.axis_size("front")
    width = lax.axis_size("col")
    fr, panel = leaf_load.shape
    sep = leaf_coupling.shape[0]
    block = leaf_inverse.shape[0]
    tile = surface_coupling.shape[1]
    half, quarter = panel // 2, panel // 4
    r1, r2, r3 = inverse_first.shape[0], inverse_second.shape[0], inverse_third.shape[0]
    vmem = pl.BlockSpec(memory_space=pltpu.VMEM)
    hbm = pl.BlockSpec(memory_space=pl.ANY)

    def v(*shape, dtype=BF):
        return pltpu.VMEM(shape, dtype)

    results = pl.pallas_call(
        functools.partial(kernel, n),
        out_shape=[
            jax.ShapeDtypeStruct(s, BF)
            for s in ((fr, panel), (tile, panel), (r1, panel), (r2, panel), (r3, panel))
        ],
        in_specs=[hbm, vmem, hbm] + [vmem] * 12 + [hbm],
        out_specs=[vmem] * 5,
        scratch_shapes=[
            v(block * width, fr), v(fr, sep), v(fr, panel), v(sep, panel, dtype=F32),
            v(2, 2 * r1, sep), v(4, 2 * r2, sep), v(8, r3, sep),
            v(sep, half), v(sep, half), v(sep, half),
            v(fr, panel), v(sep, fr),
            v(2, sep, quarter), v(2, sep, quarter), v(2, sep, quarter), v(2, sep, quarter),
            v(2, sep, quarter), v(2, sep, quarter), v(2, sep, quarter), v(2, sep, quarter),
            v(sep, half), v(sep, half), v(2, 2, sep, quarter),
            v(2, r3, half), v(2, r2, half), v(fr, half), v(2, fr, half),
            v(*surface_coupling.shape), v(2, 4, tile, half), v(2, 3, tile, half), v(2, tile, half),
            pltpu.SemaphoreType.DMA((64,)), pltpu.SemaphoreType.DMA((64,)),
            pltpu.SemaphoreType.DMA((2, 4, tile // block)),
            pltpu.SemaphoreType.DMA((2, 4, tile // block)),
            pltpu.SemaphoreType.DMA((3,)),
        ],
        compiler_params=pltpu.CompilerParams(
            collective_id=0, has_side_effects=True, vmem_limit_bytes=56 * 1024 * 1024
        ),
        cost_estimate=pl.CostEstimate(
            flops=12 * fr * fr * panel, bytes_accessed=16 * fr * fr, transcendentals=0
        ),
    )(
        leaf_load, leaf_inverse, leaf_coupling, leaf_rowmap,
        load_first, load_second, load_third,
        inverse_first, inverse_second, inverse_third,
        coupling_first, coupling_second, rowmap_first, rowmap_second, neighbor_tiles.T,
        surface_coupling,
    )
    return pl.pallas_call(
        hand_over,
        out_shape=[jax.ShapeDtypeStruct(x.shape, x.dtype) for x in results],
        in_specs=[hbm] * 5,
        out_specs=[hbm] * 5,
        scratch_shapes=[v(*x.shape) for x in results]
        + [pltpu.SemaphoreType.DMA((5,)), pltpu.SemaphoreType.DMA((5,))],
        compiler_params=pltpu.CompilerParams(vmem_limit_bytes=60 * 1024 * 1024),
    )(*results)


def solution(mesh):
    return jax.shard_map(
        local,
        mesh=mesh,
        in_specs=(
            P("front", "col"), P(("front", "col"), None), P("front", None), P("front", None),
            P("front", "col"), P("front", "col"), P("front", "col"),
            P("front", None), P("front", None), P("front", None),
            P(None, "front"), P(None, "front"), P(), P(),
            P("front", None, None), P(),
        ),
        out_specs=(P("front", "col"),) * 5,
        check_vma=False,
    )
```
